32 devices in a mesh: grp: 2 (over y), tm: 8 (over z, x), apa: 2 (over core).
Axes of the slice: x: 2, y: 2, z: 4, core: 2. Of those that a mesh axis runs over, the one named last changes fastest.
Arguments:
- waveforms: bfloat16 [5120, 2048], P(('grp', 'apa'), 'tm'), parts along dimension 0, may hold values from -6 to 6
- time_kernel: bfloat16 [3, 64], replicated, may hold values from -0.75 to 0.75
- wire_slot: int32 [5120], P('grp'), parts along dimension 0, may hold values from 0 to 2559, each once
- tick_offset: int32 [5120], P('grp'), parts along dimension 0, may hold values from 0 to 63
- bad_channel: int32 [5120], P('grp'), parts along dimension 0, may hold values 0 or 1
- induction_real: float32 [2, 800], replicated, may hold values from 0.5 to 2
- induction_imaginary: float32 [2, 800], replicated, may hold values from -1 to 1
- induction_filter: float32 [2, 800], replicated, may hold values from 0.2 to 1
- collection_real: float32 [960], replicated, may hold values from 0.5 to 2
- collection_imaginary: float32 [960], replicated, may hold values from -1 to 1
- collection_filter: float32 [960], replicated, may hold values from 0.2 to 1
Outputs:
- deconvolved: float32 [5120, 2048], P('grp', ('tm', 'apa')), parts along dimension 0
The draws below stay inside these ranges and needn't reach their ends.
There are 2 independent parts, one for each index of `grp`. The reference program is written for one: setup_inputs(seed, part) draws one part's arguments, and reference() takes and returns one part's arrays. A program takes and returns all parts, laid end to end along the dimension named above; an argument that names none is the same for every part. Nothing has to cross between parts.
Inputs may be any that keep to these rules, and one draw needn't show every extreme that they name: A permutation: readout channel c is slot wire_slot[c] of the plane layout, whose assemblies hold 2560 slots each, U wires first, then V, then W. `bad_channel`: 1 marks a bad channel.
All inputs are finite; a program needn't handle non-finite values.
Results may differ from the reference program's by a relative error of at most 0.0051.
Values may be sent and summed in bfloat16 or wider, within the bound.
A program may use at most 64 MiB of HBM per device.

```python
import math
import jax
import jax.numpy as jnp
from jax import lax

INDUCTION_WIRES = 800
COLLECTION_WIRES = 960
KERNEL_TAPS = 64
OFFSET_RANGE = 64
CHANNELS = 2560
TICKS = 2048


def touch_ends(values, key, low, high):
    dims = values.shape
    spot = [jax.random.randint(jax.random.fold_in(key, axis), (), 0, dims[axis]) for axis in range(len(dims))]
    values = values.at[tuple(spot)].set(low)
    longest = dims.index(max(dims))
    spot[longest] = (spot[longest] + 1) % dims[longest]
    return values.at[tuple(spot)].set(high)


def level_of(key, extent, pieces, low, high):
    factor_of, own = 1.0, jax.random.fold_in(key, 6)
    for position, shards_of in pieces:
        heights = jnp.exp(jax.random.uniform(jax.random.fold_in(own, position), (shards_of,), jnp.float32, low / len(pieces), high / len(pieces)))
        factor_of = factor_of * jnp.repeat(heights, extent[position] // shards_of).reshape([-1 if axis == position else 1 for axis in range(len(extent))])
    return factor_of


def centred(rng, shape, spread, most, shards=(), held_as=jnp.bfloat16):
    entries = jax.random.normal(rng, shape, jnp.float32) * spread
    if len(shards) > 0:
        entries = level_of(rng, shape, shards, -0.22, 0.18) * entries
    return jnp.clip(entries, min=-most, max=most).astype(held_as)


def setup_inputs(seed: int = 0, part: int = 0) -> dict:
    arg_keys = jax.random.split(jax.random.key(seed), 12)
    part_splits = jax.random.split(jax.random.fold_in(arg_keys[11], part), 12)
    waveforms = centred(part_splits[0], (CHANNELS, TICKS), 1.0, 6.0, ((0, 2), (1, 8)))
    time_kernel = centred(arg_keys[1], (3, KERNEL_TAPS), KERNEL_TAPS ** -0.5, 0.75)
    wire_slot = jax.random.permutation(part_splits[2], CHANNELS).astype(jnp.int32)
    tick_offset = touch_ends(jax.random.randint(part_splits[3], (CHANNELS,), 0, OFFSET_RANGE), jax.random.fold_in(part_splits[3], 1), 0, OFFSET_RANGE - 1).astype(jnp.int32)
    bad_channel = touch_ends((jax.random.randint(part_splits[4], (CHANNELS,), 0, 16) < 1).astype(jnp.int32), jax.random.fold_in(part_splits[4], 1), 0, 1)
    induction_real = jnp.clip(jax.random.uniform(arg_keys[5], (2, INDUCTION_WIRES), jnp.float32, 0.5, 2.0), 0.5, 2.0)
    induction_imaginary = jnp.clip(jax.random.uniform(arg_keys[6], (2, INDUCTION_WIRES), jnp.float32, -1.0, 1.0), -1.0, 1.0)
    induction_filter = jnp.clip(jnp.exp(jax.random.uniform(arg_keys[7], (2, INDUCTION_WIRES), jnp.float32, math.log(0.2), math.log(1.0))), 0.2, 1.0)
    collection_real = jnp.clip(jax.random.uniform(arg_keys[8], (COLLECTION_WIRES,), jnp.float32, 0.5, 2.0), 0.5, 2.0)
    collection_imaginary = jnp.clip(jax.random.uniform(arg_keys[9], (COLLECTION_WIRES,), jnp.float32, -1.0, 1.0), -1.0, 1.0)
    collection_filter = jnp.clip(jnp.exp(jax.random.uniform(arg_keys[10], (COLLECTION_WIRES,), jnp.float32, math.log(0.2), math.log(1.0))), 0.2, 1.0)
    return dict(waveforms=waveforms, time_kernel=time_kernel, wire_slot=wire_slot, tick_offset=tick_offset, bad_channel=bad_channel, induction_real=induction_real, induction_imaginary=induction_imaginary, induction_filter=induction_filter, collection_real=collection_real, collection_imaginary=collection_imaginary, collection_filter=collection_filter)


def slot_plane(slot_index):
    assembly_wires = 2 * INDUCTION_WIRES + COLLECTION_WIRES
    within = slot_index % assembly_wires
    return (within >= INDUCTION_WIRES).astype(jnp.int32) + (within >= 2 * INDUCTION_WIRES).astype(jnp.int32)


def fourier_tables(wire_count):
    positions = jnp.arange(wire_count, dtype=jnp.int32)
    phase_turns = (positions[:, None] * positions[None, :]) % wire_count
    phase_angle = phase_turns.astype(jnp.float32) * (2.0 * math.pi / wire_count)
    cosine = jnp.cos(phase_angle).astype(jnp.bfloat16)
    sine_table = jnp.sin(phase_angle).astype(jnp.bfloat16)
    forward = jnp.concatenate([cosine, sine_table], 0)
    backward = jnp.concatenate([cosine, -sine_table], 1)
    return forward, backward


def wire_deconvolve(plane_rows, tables, response_real, response_imaginary, filter_gain):
    forward, backward = tables
    wire_count = plane_rows.shape[0]
    magnitude = response_real * response_real + response_imaginary * response_imaginary
    ratio_real = (filter_gain * response_real / magnitude)[:, None]
    ratio_imaginary = (-filter_gain * response_imaginary / magnitude)[:, None]
    signal = lax.optimization_barrier(plane_rows).astype(jnp.float32)
    spectrum = jnp.dot(forward.astype(jnp.float32), signal, preferred_element_type=jnp.float32, precision=lax.Precision.HIGHEST)
    cosine_part = spectrum[:wire_count]
    sine_part = spectrum[wire_count:]
    product = jnp.concatenate([cosine_part * ratio_real + sine_part * ratio_imaginary, cosine_part * ratio_imaginary - sine_part * ratio_real], 0)
    product = lax.optimization_barrier(product.astype(jnp.bfloat16)).astype(jnp.float32)
    result = jnp.dot(backward.astype(jnp.float32), product, preferred_element_type=jnp.float32, precision=lax.Precision.HIGHEST)
    return result * (1.0 / wire_count)


def deconvolve_planes(ordered, induction_real, induction_imaginary, induction_filter, collection_real, collection_imaginary, collection_filter):
    assembly_wires = 2 * INDUCTION_WIRES + COLLECTION_WIRES
    induction_tables = fourier_tables(INDUCTION_WIRES)
    collection_tables = fourier_tables(COLLECTION_WIRES)
    results = []
    for assembly in range(ordered.shape[0] // assembly_wires):
        first_row = assembly * assembly_wires
        for plane_index in range(2):
            row_start = first_row + plane_index * INDUCTION_WIRES
            results.append(wire_deconvolve(ordered[row_start:row_start + INDUCTION_WIRES], induction_tables, induction_real[plane_index], induction_imaginary[plane_index], induction_filter[plane_index]))
        row_start = first_row + 2 * INDUCTION_WIRES
        results.append(wire_deconvolve(ordered[row_start:row_start + COLLECTION_WIRES], collection_tables, collection_real, collection_imaginary, collection_filter))
    return jnp.concatenate(results, 0)


def time_filter(waveforms, time_kernel, wire_slot, tick_offset, bad_channel):
    tick_count = waveforms.shape[1]
    channel_count = waveforms.shape[0]
    kernel_spectrum = jnp.fft.rfft(time_kernel.astype(jnp.float32), n=tick_count, axis=1)
    frequency = jnp.arange(tick_count // 2 + 1, dtype=jnp.int32)
    block_rows = math.gcd(channel_count, 128)
    block_count = channel_count // block_rows
    plane_ids = slot_plane(wire_slot)
    keep_factor = (1 - bad_channel).astype(jnp.float32)

    def filter_block(inputs):
        signal, planes_here, offsets, kept_rows = inputs
        spectrum = jnp.fft.rfft(signal.astype(jnp.float32) * kept_rows[:, None], axis=1)
        phase_turns = (frequency[None, :] * offsets[:, None]) % tick_count
        phase_angle = phase_turns.astype(jnp.float32) * (2.0 * math.pi / tick_count)
        rotated = spectrum * jnp.exp(-1j * phase_angle) * kernel_spectrum[planes_here]
        return jnp.fft.irfft(rotated, n=tick_count, axis=1).astype(jnp.bfloat16)

    inputs = (waveforms.reshape(block_count, block_rows, tick_count), plane_ids.reshape(block_count, block_rows), tick_offset.reshape(block_count, block_rows), keep_factor.reshape(block_count, block_rows))
    return lax.map(filter_block, inputs).reshape(channel_count, tick_count)


def reference(waveforms, time_kernel, wire_slot, tick_offset, bad_channel, induction_real, induction_imaginary, induction_filter, collection_real, collection_imaginary, collection_filter):
    filtered = time_filter(waveforms, time_kernel, wire_slot, tick_offset, bad_channel)
    channel_count = wire_slot.shape[0]
    inverse = jnp.zeros((channel_count,), jnp.int32).at[wire_slot].set(jnp.arange(channel_count, dtype=jnp.int32))
    ordered = filtered[inverse]
    return deconvolve_planes(ordered, induction_real, induction_imaginary, induction_filter, collection_real, collection_imaginary, collection_filter)
```

```python
import math

import jax
import jax.numpy as jnp
import ml_dtypes
import numpy as np
from jax import lax
from jax.sharding import PartitionSpec as P

INDUCTION_WIRES = 800
COLLECTION_WIRES = 960
OFFSET_RANGE = 64


def shifted(value, axis, steps):
    count = lax.axis_size(axis)
    pairs = [(source, (source + steps) % count) for source in range(count)]
    return lax.ppermute(value, axis, pairs)


def slot_plane(slot_index):
    assembly_wires = 2 * INDUCTION_WIRES + COLLECTION_WIRES
    within = slot_index % assembly_wires
    return (within >= INDUCTION_WIRES).astype(jnp.int32) + (within >= 2 * INDUCTION_WIRES).astype(
        jnp.int32
    )


def fourier_tables(wire_count):
    positions = np.arange(wire_count, dtype=np.int64)
    phase_turns = positions[:, None] * positions[None, :] % wire_count
    phase_angle = phase_turns * (2.0 * math.pi / wire_count)
    cosine = np.cos(phase_angle).astype(ml_dtypes.bfloat16)
    sine_table = np.sin(phase_angle).astype(ml_dtypes.bfloat16)
    forward = np.concatenate([cosine, sine_table], 0)
    backward = np.concatenate([cosine, -sine_table], 1)
    return (forward, backward)


def wire_deconvolve(plane_rows, tables, response_real, response_imaginary, filter_gain):
    forward, backward = tables
    wire_count = plane_rows.shape[0]
    magnitude = response_real * response_real + response_imaginary * response_imaginary
    ratio_real = (filter_gain * response_real / magnitude)[:, None]
    ratio_imaginary = (-filter_gain * response_imaginary / magnitude)[:, None]
    spectrum = jnp.dot(forward, plane_rows, preferred_element_type=jnp.float32)
    cosine_part = spectrum[:wire_count]
    sine_part = spectrum[wire_count:]
    product = jnp.concatenate(
        [
            cosine_part * ratio_real + sine_part * ratio_imaginary,
            cosine_part * ratio_imaginary - sine_part * ratio_real,
        ],
        0,
    ).astype(jnp.bfloat16)
    return jnp.dot(backward, product, preferred_element_type=jnp.float32) * (1.0 / wire_count)


def deconvolve_planes(
    ordered,
    induction_real,
    induction_imaginary,
    induction_filter,
    collection_real,
    collection_imaginary,
    collection_filter,
):
    induction_tables = fourier_tables(INDUCTION_WIRES)
    collection_tables = fourier_tables(COLLECTION_WIRES)
    results = []
    for plane_index in range(2):
        row_start = plane_index * INDUCTION_WIRES
        results.append(
            wire_deconvolve(
                ordered[row_start : row_start + INDUCTION_WIRES],
                induction_tables,
                induction_real[plane_index],
                induction_imaginary[plane_index],
                induction_filter[plane_index],
            )
        )
    row_start = 2 * INDUCTION_WIRES
    results.append(
        wire_deconvolve(
            ordered[row_start : row_start + COLLECTION_WIRES],
            collection_tables,
            collection_real,
            collection_imaginary,
            collection_filter,
        )
    )
    return jnp.concatenate(results, 0)


def toeplitz(kernel_row):
    tap_count = kernel_row.shape[0]
    padded = jnp.concatenate(
        [
            jnp.zeros((tap_count - 1,), kernel_row.dtype),
            kernel_row,
            jnp.zeros((tap_count,), kernel_row.dtype),
        ]
    )
    padded_length = padded.shape[0]
    rolled = jnp.roll(padded, 1 - 2 * tap_count)
    tiled = jnp.tile(rolled, 2 * tap_count)[: 2 * tap_count * (padded_length - 1)]
    return tiled.reshape(2 * tap_count, padded_length - 1)[:, :tap_count]


def shift_rows(extended, offsets, length):
    current = extended
    for bit_number in range((OFFSET_RANGE - 1).bit_length()):
        step_ticks = 1 << bit_number
        moved = jnp.concatenate(
            [jnp.zeros((current.shape[0], step_ticks), current.dtype), current[:, :-step_ticks]], 1
        )
        chosen = offsets >> bit_number & 1 == 1
        current = jnp.where(chosen[:, None], moved, current)
    return current[:, OFFSET_RANGE : OFFSET_RANGE + length]


def convolve(aligned, table, tap_count):
    row_count = aligned.shape[0]
    blocks = aligned.reshape(row_count, aligned.shape[1] // tap_count, tap_count)
    result = jnp.einsum(
        "cjq,qr->cjr", blocks[:, :-1], table[:tap_count], preferred_element_type=jnp.float32
    )
    result = result + jnp.einsum(
        "cjq,qr->cjr", blocks[:, 1:], table[tap_count:], preferred_element_type=jnp.float32
    )
    return result.reshape(row_count, -1)


def local(
    waveforms,
    time_kernel,
    wire_slot,
    tick_offset,
    bad_channel,
    induction_real,
    induction_imaginary,
    induction_filter,
    collection_real,
    collection_imaginary,
    collection_filter,
):
    tap_count = time_kernel.shape[1]
    tail_ticks = tap_count + OFFSET_RANGE
    channel_count = wire_slot.shape[0]
    inverse = (
        jnp.zeros((channel_count,), jnp.int32)
        .at[wire_slot]
        .set(jnp.arange(channel_count, dtype=jnp.int32))
    )
    tables = [toeplitz(time_kernel[plane_index]) for plane_index in range(3)]
    row_count = waveforms.shape[0]
    first_row = lax.axis_index("apa") * row_count
    local_offset = lax.dynamic_slice_in_dim(tick_offset, first_row, row_count)
    local_bad = lax.dynamic_slice_in_dim(bad_channel, first_row, row_count)
    local_plane = slot_plane(lax.dynamic_slice_in_dim(wire_slot, first_row, row_count))
    masked = waveforms * (1 - local_bad).astype(jnp.bfloat16)[:, None]
    earlier = shifted(masked[:, -tail_ticks:], "tm", 1)
    aligned = shift_rows(
        jnp.concatenate([earlier, masked], 1), local_offset, masked.shape[1] + tap_count
    )
    summed = jnp.zeros(masked.shape, jnp.float32)
    for plane_index in range(3):
        summed = summed + jnp.where(
            (local_plane == plane_index)[:, None],
            convolve(aligned, tables[plane_index], tap_count),
            0.0,
        )
    filtered = summed.astype(jnp.bfloat16)
    regrouped = lax.all_to_all(filtered, "apa", split_axis=1, concat_axis=0, tiled=True)
    ordered = regrouped[inverse]
    return deconvolve_planes(
        ordered,
        induction_real,
        induction_imaginary,
        induction_filter,
        collection_real,
        collection_imaginary,
        collection_filter,
    )


def solution(mesh):
    placed = (
        P(("grp", "apa"), "tm"),
        P(),
        P("grp"),
        P("grp"),
        P("grp"),
        P(),
        P(),
        P(),
        P(),
        P(),
        P(),
    )
    return jax.shard_map(
        local, mesh=mesh, in_specs=placed, out_specs=P("grp", ("tm", "apa")), check_vma=False
    )
```

```python
import functools
import math

import jax
import jax.numpy as jnp
import numpy as np
from jax import lax
from jax.experimental import pallas as pl
from jax.experimental.pallas import tpu as pltpu
from jax.sharding import PartitionSpec as P

LANES = 128
CHUNK = 256
MESH = pl.DeviceIdType.MESH
HIGHEST = lax.Precision.HIGHEST


def rounded_up(count):
    return -(-count // LANES) * LANES


def phase_tables(wire_count):
    padded = rounded_up(wire_count)
    columns = (padded - np.arange(2 * padded)) % wire_count
    multiples = np.concatenate([np.arange(LANES), LANES * np.arange(8)])
    turns = multiples[:, None] * columns[None, :] % wire_count
    angle = turns * (2.0 * math.pi / wire_count)
    return np.concatenate([np.cos(angle), np.sin(angle)], 1).astype(np.float32)


def strided(row):
    return pltpu.roll(jnp.broadcast_to(row, (LANES, LANES)), 0, 1, stride=1, stride_axis=0)


def kernel(
    induction,
    collection,
    waves,
    taps,
    slots,
    offsets,
    bad,
    induction_real,
    induction_imaginary,
    induction_filter,
    collection_real,
    collection_imaginary,
    collection_filter,
    induction_phases,
    collection_phases,
    out,
    halo,
    main,
    onehot,
    total,
    circulant_u,
    circulant_v,
    circulant_w,
    phases_uv,
    phases_w,
    spread,
    folded,
    rows_h,
    kernel_rows,
    result,
    next_send,
    near_send,
    far_send,
    halo_sem,
    main_sem,
    table_sem,
    out_sem,
):
    tm, apa = lax.axis_index("tm"), lax.axis_index("apa")
    windows = lax.axis_size("tm")
    following = lax.rem(tm + 1, windows)
    previous = lax.rem(tm + windows - 1, windows)
    pieces = waves.shape[0] // CHUNK
    padded_i, padded_c = rounded_up(induction), rounded_up(collection)
    bases = (0, padded_i, 2 * padded_i)
    sizes = (induction, induction, collection)

    barrier = pltpu.get_barrier_semaphore()

    def greet(window, core):
        pl.semaphore_signal(
            barrier, inc=1, device_id={"tm": window, "apa": core}, device_id_type=MESH
        )

    greet(tm, 1 - apa)

    @pl.when(apa == 0)
    def _():
        greet(previous, 0)
        greet(previous, 1)

    tables = [
        pltpu.make_async_copy(induction_phases, phases_uv, table_sem.at[0]),
        pltpu.make_async_copy(collection_phases, phases_w, table_sem.at[1]),
    ]
    pl.semaphore_wait(barrier, 2)

    def part(index, half):
        return waves.at[pl.ds(index * CHUNK, CHUNK), pl.ds(half * LANES, LANES)]

    def push(index, half, target, arrived, sent, window, core):
        return pltpu.make_async_remote_copy(
            src_ref=part(index, half),
            dst_ref=target,
            send_sem=sent,
            recv_sem=arrived,
            device_id={"tm": window, "apa": core},
            device_id_type=MESH,
        )

    def sends(core, kept=True):
        first = core * pieces
        ahead = [
            push(k, 1, halo.at[first + k], halo_sem.at[first + k], next_send.at[k], following, 0)
            for k in range(pieces)
        ]
        across, stay = [], []
        for k in range(pieces):
            spot = first + k
            if core == 0:
                across.append(
                    push(k, 0, halo.at[spot], halo_sem.at[spot], near_send.at[k], tm, 1)
                )
                across.append(
                    push(k, 1, main.at[spot], main_sem.at[spot], far_send.at[k], tm, 1)
                )
                kept and stay.append(pltpu.make_async_copy(part(k, 0), main.at[spot], main_sem.at[spot]))
            else:
                across.append(
                    push(k, 0, main.at[spot], main_sem.at[spot], near_send.at[k], tm, 0)
                )
                kept and stay.append(pltpu.make_async_copy(part(k, 0), halo.at[spot], halo_sem.at[spot]))
                kept and stay.append(pltpu.make_async_copy(part(k, 1), main.at[spot], main_sem.at[spot]))
        return ahead, across, stay

    for core in range(2):

        @pl.when(apa == core)
        def _():
            ahead, across, stay = sends(core)
            for copy in ahead + across + stay:
                copy.start()

    for copy in tables:
        copy.start()

    tile_rows = total.shape[0] // 11 if total.shape[0] % 11 == 0 else LANES
    lanes_row = lax.broadcasted_iota(jnp.int32, (tile_rows, CHUNK), 0)

    def make_onehot(index, carry):
        slot = slots[index]
        gap = padded_i - induction
        slot = slot + jnp.where(slot >= induction, gap, 0) + jnp.where(
            slot >= 2 * induction, gap, 0
        )
        slot = jnp.where(bad[index] == 0, slot, -1)
        for start in range(0, total.shape[0], tile_rows):
            hit = lanes_row == slot - start
            onehot[index, start : start + tile_rows, :] = jnp.where(hit, 1.0, 0.0).astype(
                jnp.bfloat16
            )
        return carry

    lax.fori_loop(0, 2 * pieces, make_onehot, 0)
    total[...] = jnp.zeros_like(total)

    spread[...] = jnp.zeros_like(spread)
    kernel_rows[...] = jnp.zeros_like(kernel_rows)
    kernel_rows[0:3, 0 : taps.shape[1]] = taps[...].astype(jnp.float32)
    for real, imaginary, gain, row in (
        (induction_real, induction_imaginary, induction_filter, 0),
        (collection_real, collection_imaginary, collection_filter, 4),
    ):
        count, width = real.shape
        re, im = real[...], imaginary[...]
        magnitude = re * re + im * im
        spread[row : row + count, 0:width] = gain[...] * re / magnitude
        spread[row + count : row + 2 * count, 0:width] = -gain[...] * im / magnitude
    for copy in tables:
        copy.wait()
    lane = lax.broadcasted_iota(jnp.int32, (LANES, LANES), 1)
    row_of = lax.broadcasted_iota(jnp.int32, (LANES, LANES), 0)
    for phases, count, first, targets, wires in (
        (phases_uv, 2, 0, (circulant_u, circulant_v), induction),
        (phases_w, 1, 4, (circulant_w,), collection),
    ):
        blocks = rounded_up(wires) // LANES
        length = 2 * blocks * LANES
        for entry in range(2 * count):
            for block in range(8):
                folded[8 * entry + block : 8 * entry + block + 1, :] = spread[
                    first + entry : first + entry + 1, block * LANES : (block + 1) * LANES
                ]
        terms = jnp.dot(
            folded[0 : 16 * count, :],
            phases[0:LANES, :],
            preferred_element_type=jnp.float32,
            precision=HIGHEST,
        )
        for entry in range(count):
            low, high = 8 * entry, 8 * (count + entry)
            re = terms[low : low + 8, :length] - terms[high : high + 8, length:]
            im = terms[low : low + 8, length:] + terms[high : high + 8, :length]
            turned = (
                phases[LANES : LANES + 8, :length] * re - phases[LANES : LANES + 8, length:] * im
            )
            rows_h[0:1, 0:length] = jnp.sum(turned, axis=0, keepdims=True) * (1.0 / wires)
            before = strided(rows_h[0:1, 0:LANES])
            for k in range(2 * blocks - 1):
                after = strided(rows_h[0:1, (k + 1) * LANES : (k + 2) * LANES])
                piece = jnp.where(lane >= row_of, after, before).astype(jnp.bfloat16)
                for i in range(blocks):
                    j = k - (blocks - 1) + i
                    if 0 <= j < blocks:
                        targets[entry][
                            i * LANES : (i + 1) * LANES, j * LANES : (j + 1) * LANES
                        ] = piece
                before = after

    def take(step, carry):
        index = lax.rem(step, 2) * pieces + step // 2
        pltpu.make_async_copy(main.at[index], main.at[index], main_sem.at[index]).wait()
        pltpu.make_async_copy(halo.at[index], halo.at[index], halo_sem.at[index]).wait()
        groups = []
        for start in range(0, CHUNK, LANES):
            delay = offsets[index, :, start : start + LANES].astype(jnp.float32)
            delay = jnp.broadcast_to(delay, (LANES, LANES)).T.astype(jnp.int32)
            origin = (lane - delay) & (LANES - 1)
            early = halo[index, start : start + LANES, :].astype(jnp.float32)
            late = main[index, start : start + LANES, :].astype(jnp.float32)
            early = jnp.take_along_axis(early, origin, axis=1)
            late = jnp.take_along_axis(late, origin, axis=1)
            late = jnp.where(lane >= delay, late, early)
            groups.append(jnp.concatenate([early, late], 1).astype(jnp.bfloat16))
        aligned = jnp.concatenate(groups, 0)
        for start in range(0, total.shape[0], tile_rows):
            total[start : start + tile_rows, :] += jnp.dot(
                onehot[index, start : start + tile_rows, :],
                aligned,
                preferred_element_type=jnp.float32,
            )
        return carry

    lax.fori_loop(0, 2 * pieces, take, 0)

    outs = []
    place = 0
    for plane, circulant in enumerate((circulant_u, circulant_v, circulant_w)):
        base, wires = bases[plane], sizes[plane]
        padded = rounded_up(wires)
        turned = strided(kernel_rows[plane : plane + 1, :])
        toeplitz = jnp.concatenate(
            [jnp.where(lane < row_of, turned, 0.0), jnp.where(lane >= row_of, turned, 0.0)], 0
        ).astype(jnp.bfloat16)
        filtered = jnp.dot(
            total[base : base + padded, :].astype(jnp.bfloat16),
            toeplitz,
            preferred_element_type=jnp.float32,
        ).astype(jnp.bfloat16)
        values = jnp.dot(circulant[...], filtered, preferred_element_type=jnp.float32)
        result[place : place + wires, :] = values[:wires]
        span = pl.ds(place, wires)
        outs.append(pltpu.make_async_copy(result.at[span], out.at[span], out_sem.at[plane]))
        outs[-1].start()
        place += wires
    for copy in outs:
        copy.wait()
    for core in range(2):

        @pl.when(apa == core)
        def _():
            ahead, across, stay = sends(core, False)
            for copy in ahead + across:
                copy.wait_send()


def local(
    waveforms,
    time_kernel,
    wire_slot,
    tick_offset,
    bad_channel,
    induction_real,
    induction_imaginary,
    induction_filter,
    collection_real,
    collection_imaginary,
    collection_filter,
):
    channels = wire_slot.shape[0]
    induction, collection = induction_real.shape[1], collection_real.shape[0]
    padded_i, padded_c = rounded_up(induction), rounded_up(collection)
    rows = 2 * padded_i + padded_c
    chunks = channels // CHUNK
    pieces = chunks // 2
    vmem, anywhere = pl.BlockSpec(memory_space=pltpu.VMEM), pl.BlockSpec(memory_space=pl.ANY)
    uv, w = phase_tables(induction), phase_tables(collection)
    return pl.pallas_call(
        functools.partial(kernel, induction, collection),
        out_shape=jax.ShapeDtypeStruct((channels, LANES), jnp.float32),
        in_specs=[anywhere] + [vmem] * 10 + [anywhere] * 2,
        out_specs=anywhere,
        scratch_shapes=[
            pltpu.VMEM((chunks, CHUNK, LANES), jnp.bfloat16),
            pltpu.VMEM((chunks, CHUNK, LANES), jnp.bfloat16),
            pltpu.VMEM((chunks, rows, CHUNK), jnp.bfloat16),
            pltpu.VMEM((rows, 2 * LANES), jnp.float32),
            pltpu.VMEM((padded_i, padded_i), jnp.bfloat16),
            pltpu.VMEM((padded_i, padded_i), jnp.bfloat16),
            pltpu.VMEM((padded_c, padded_c), jnp.bfloat16),
            pltpu.VMEM(uv.shape, jnp.float32),
            pltpu.VMEM(w.shape, jnp.float32),
            pltpu.VMEM((8, 8 * LANES), jnp.float32),
            pltpu.VMEM((32, LANES), jnp.float32),
            pltpu.VMEM((8, 2 * max(padded_i, padded_c)), jnp.float32),
            pltpu.VMEM((8, LANES), jnp.float32),
            pltpu.VMEM((channels, LANES), jnp.float32),
            pltpu.SemaphoreType.DMA((pieces,)),
            pltpu.SemaphoreType.DMA((pieces,)),
            pltpu.SemaphoreType.DMA((pieces,)),
            pltpu.SemaphoreType.DMA((chunks,)),
            pltpu.SemaphoreType.DMA((chunks,)),
            pltpu.SemaphoreType.DMA((2,)),
            pltpu.SemaphoreType.DMA((3,)),
        ],
        compiler_params=pltpu.CompilerParams(
            collective_id=0, has_side_effects=True, vmem_limit_bytes=48 * 1024 * 1024
        ),
    )(
        waveforms,
        time_kernel,
        wire_slot.reshape(chunks, 1, CHUNK),
        tick_offset.reshape(chunks, 1, CHUNK),
        bad_channel.reshape(chunks, 1, CHUNK),
        induction_real,
        induction_imaginary,
        induction_filter,
        collection_real.reshape(1, collection),
        collection_imaginary.reshape(1, collection),
        collection_filter.reshape(1, collection),
        uv,
        w,
    )


def solution(mesh):
    placed = (
        P(("grp", "apa"), "tm"),
        P(),
        P("grp"),
        P("grp"),
        P("grp"),
        P(),
        P(),
        P(),
        P(),
        P(),
        P(),
    )
    return jax.shard_map(
        local, mesh=mesh, in_specs=placed, out_specs=P("grp", ("tm", "apa")), check_vma=False
    )
```

```python
import functools
import math

import jax
import jax.numpy as jnp
import numpy as np
from jax import lax
from jax.experimental import pallas as pl
from jax.experimental.pallas import tpu as pltpu
from jax.sharding import PartitionSpec as P

LANES = 128
CHUNK = 256
MESH = pl.DeviceIdType.MESH


def rounded_up(count):
    return -(-count // LANES) * LANES


def phase_tables(wire_count):
    padded = rounded_up(wire_count)
    columns = (padded - np.arange(padded)) % wire_count

    def both(multiples):
        angle = (multiples[:, None] * columns[None, :] % wire_count) * (2.0 * math.pi / wire_count)
        return np.concatenate([np.cos(angle), np.sin(angle)], 0)

    fine, coarse = both(np.arange(LANES)), both(LANES * np.arange(8))
    return fine.astype(np.float32), coarse.astype(np.float32)


def halves(values):
    high = values.astype(jnp.bfloat16)
    return high, (values - high.astype(jnp.float32)).astype(jnp.bfloat16)


def strided(row):
    return pltpu.roll(jnp.broadcast_to(row, (LANES, LANES)), 0, 1, stride=1, stride_axis=0)


def kernel(induction, collection, waves, *refs):
    operands, out, copies = refs[:14], refs[14], refs[15:29]
    (
        halo,
        main,
        onehot,
        total,
        circulant_u,
        circulant_v,
        circulant_w,
        spread,
        folded,
        rows_h,
        kernel_rows,
        result,
        next_send,
        near_send,
        far_send,
        halo_sem,
        main_sem,
        fetch_sem,
        out_sem,
    ) = refs[29:]
    (
        taps,
        slots,
        offsets,
        bad,
        induction_real,
        induction_imaginary,
        induction_filter,
        collection_real,
        collection_imaginary,
        collection_filter,
        fine_uv,
        coarse_uv,
        fine_w,
        coarse_w,
    ) = copies
    tm, apa = lax.axis_index("tm"), lax.axis_index("apa")
    windows = lax.axis_size("tm")
    following = lax.rem(tm + 1, windows)
    previous = lax.rem(tm + windows - 1, windows)
    pieces = waves.shape[0] // CHUNK
    padded_i, padded_c = rounded_up(induction), rounded_up(collection)
    bases = (0, padded_i, 2 * padded_i)
    sizes = (induction, induction, collection)

    barrier = pltpu.get_barrier_semaphore()

    def greet(window, core):
        pl.semaphore_signal(
            barrier, inc=1, device_id={"tm": window, "apa": core}, device_id_type=MESH
        )

    greet(tm, 1 - apa)

    @pl.when(apa == 0)
    def _():
        greet(previous, 0)
        greet(previous, 1)

    fetches = [
        pltpu.make_async_copy(source, copy, fetch_sem.at[number])
        for number, (source, copy) in enumerate(zip(operands, copies))
    ]
    for fetch in fetches[:10]:
        fetch.start()
    pl.semaphore_wait(barrier, 2)

    def part(index, half):
        return waves.at[pl.ds(index * CHUNK, CHUNK), pl.ds(half * LANES, LANES)]

    def push(index, half, target, arrived, sent, window, core):
        return pltpu.make_async_remote_copy(
            src_ref=part(index, half),
            dst_ref=target,
            send_sem=sent,
            recv_sem=arrived,
            device_id={"tm": window, "apa": core},
            device_id_type=MESH,
        )

    def sends(core, kept=True):
        first = core * pieces
        ahead = [
            push(k, 1, halo.at[first + k], halo_sem.at[first + k], next_send.at[k], following, 0)
            for k in range(pieces)
        ]
        across, stay = [], []
        for k in range(pieces):
            spot = first + k
            if core == 0:
                across.append(
                    push(k, 0, halo.at[spot], halo_sem.at[spot], near_send.at[k], tm, 1)
                )
                across.append(
                    push(k, 1, main.at[spot], main_sem.at[spot], far_send.at[k], tm, 1)
                )
                kept and stay.append(pltpu.make_async_copy(part(k, 0), main.at[spot], main_sem.at[spot]))
            else:
                across.append(
                    push(k, 0, main.at[spot], main_sem.at[spot], near_send.at[k], tm, 0)
                )
                kept and stay.append(pltpu.make_async_copy(part(k, 0), halo.at[spot], halo_sem.at[spot]))
                kept and stay.append(pltpu.make_async_copy(part(k, 1), main.at[spot], main_sem.at[spot]))
        return ahead, across, stay

    for core in range(2):

        @pl.when(apa == core)
        def _():
            ahead, across, stay = sends(core)
            for copy in ahead + across + stay:
                copy.start()

    for fetch in fetches[10:]:
        fetch.start()
    for fetch in fetches[:10]:
        fetch.wait()

    build_rows = math.gcd(total.shape[0], 256)
    counted = lax.broadcasted_iota(jnp.int32, (build_rows, 2 * CHUNK), 0).astype(jnp.int16)
    one, zero = jnp.bfloat16(1), jnp.bfloat16(0)

    def span_of(ref, first, count):
        return ref[:, pl.ds(pl.multiple_of(first, LANES), count)]

    def joined(ref, step):
        return jnp.concatenate(
            [span_of(ref, index * CHUNK, CHUNK) for index in (step, pieces + step)], 1
        )

    def make_onehot(step, carry):
        slot = joined(slots, step)
        gap = padded_i - induction
        slot = slot + jnp.where(slot >= induction, gap, 0) + jnp.where(
            slot >= 2 * induction, gap, 0
        )
        slot = jnp.where(joined(bad, step) == 0, slot, -1)
        for start in range(0, total.shape[0], build_rows):
            hit = counted == (slot - start).astype(jnp.int16)
            onehot[step, start : start + build_rows, :] = jnp.where(hit, one, zero)
        return carry

    lax.fori_loop(0, pieces, make_onehot, 0)
    total[...] = jnp.zeros_like(total)

    spread[...] = jnp.zeros_like(spread)
    kernel_rows[...] = jnp.zeros_like(kernel_rows)
    kernel_rows[0:3, 0 : taps.shape[1]] = taps[...].astype(jnp.float32)
    for real, imaginary, gain, row in (
        (induction_real, induction_imaginary, induction_filter, 0),
        (collection_real, collection_imaginary, collection_filter, 4),
    ):
        count, width = real.shape
        re, im = real[...], imaginary[...]
        magnitude = re * re + im * im
        spread[row : row + count, 0:width] = gain[...] * re / magnitude
        spread[row + count : row + 2 * count, 0:width] = -gain[...] * im / magnitude
    for fetch in fetches[10:]:
        fetch.wait()
    lane = lax.broadcasted_iota(jnp.int32, (LANES, LANES), 1)
    row_of = lax.broadcasted_iota(jnp.int32, (LANES, LANES), 0)
    for fine, coarse, count, first, targets, wires in (
        (fine_uv, coarse_uv, 2, 0, (circulant_u, circulant_v), induction),
        (fine_w, coarse_w, 1, 4, (circulant_w,), collection),
    ):
        padded = rounded_up(wires)
        blocks = padded // LANES
        for entry in range(count):
            for block in range(8):
                columns = slice(block * LANES, (block + 1) * LANES)
                re = spread[first + entry : first + entry + 1, columns]
                im = spread[first + count + entry : first + count + entry + 1, columns]
                row = 16 * entry + block
                folded[row : row + 1, 0:LANES] = re
                folded[row : row + 1, LANES : 2 * LANES] = -im
                folded[row + 8 : row + 9, 0:LANES] = im
                folded[row + 8 : row + 9, LANES : 2 * LANES] = re
        both = jnp.concatenate(halves(folded[0 : 16 * count, :]), 0)
        terms = sum(
            jnp.dot(both, table, preferred_element_type=jnp.float32) for table in halves(fine[...])
        )
        terms = terms[: 16 * count] + terms[16 * count :]
        for entry in range(count):
            re = terms[16 * entry : 16 * entry + 8]
            im = terms[16 * entry + 8 : 16 * entry + 16]
            turned = coarse[0:8, :] * re - coarse[8:16, :] * im
            line = jnp.sum(turned, axis=0, keepdims=True) * (1.0 / wires)
            rows_h[0:1, 0:padded] = line
            rows_h[0:1, wires : wires + padded] = line
            if padded > wires:
                rows_h[0:1, 2 * wires : 2 * padded] = line[:, : 2 * (padded - wires)]
            before = strided(rows_h[0:1, 0:LANES])
            for k in range(2 * blocks - 1):
                after = strided(rows_h[0:1, (k + 1) * LANES : (k + 2) * LANES])
                piece = jnp.where(lane >= row_of, after, before).astype(jnp.bfloat16)
                for i in range(blocks):
                    j = k - (blocks - 1) + i
                    if 0 <= j < blocks:
                        targets[entry][
                            i * LANES : (i + 1) * LANES, j * LANES : (j + 1) * LANES
                        ] = piece
                before = after

    tile_rows = total.shape[0] // 2

    def take(step, carry):
        groups = []
        for index in (step, pieces + step):
            pltpu.make_async_copy(main.at[index], main.at[index], main_sem.at[index]).wait()
            pltpu.make_async_copy(halo.at[index], halo.at[index], halo_sem.at[index]).wait()
        for index in (step, pieces + step):
            for start in range(0, CHUNK, LANES):
                delay = span_of(offsets, index * CHUNK + start, LANES).astype(jnp.float32)
                delay = jnp.broadcast_to(delay, (LANES, LANES)).T.astype(jnp.int32)
                origin = (lane - delay) & (LANES - 1)
                early = halo[index, start : start + LANES, :].astype(jnp.float32)
                late = main[index, start : start + LANES, :].astype(jnp.float32)
                early = jnp.take_along_axis(early, origin, axis=1)
                late = jnp.take_along_axis(late, origin, axis=1)
                late = jnp.where(lane >= delay, late, early)
                groups.append(jnp.concatenate([early, late], 1).astype(jnp.bfloat16))
        aligned = jnp.concatenate(groups, 0)
        for start in range(0, total.shape[0], tile_rows):
            total[start : start + tile_rows, :] += jnp.dot(
                onehot[step, start : start + tile_rows, :],
                aligned,
                preferred_element_type=jnp.float32,
            )
        return carry

    lax.fori_loop(0, pieces, take, 0)

    outs = []
    place = 0
    for plane, circulant in enumerate((circulant_u, circulant_v, circulant_w)):
        base, wires = bases[plane], sizes[plane]
        padded = rounded_up(wires)
        turned = strided(kernel_rows[plane : plane + 1, :])
        toeplitz = jnp.concatenate(
            [jnp.where(lane < row_of, turned, 0.0), jnp.where(lane >= row_of, turned, 0.0)], 0
        ).astype(jnp.bfloat16)
        filtered = jnp.dot(
            total[base : base + padded, :].astype(jnp.bfloat16),
            toeplitz,
            preferred_element_type=jnp.float32,
        ).astype(jnp.bfloat16)
        values = jnp.dot(circulant[...], filtered, preferred_element_type=jnp.float32)
        result[place : place + wires, :] = values[:wires]
        span = pl.ds(place, wires)
        outs.append(pltpu.make_async_copy(result.at[span], out.at[span], out_sem.at[plane]))
        outs[-1].start()
        place += wires
    for copy in outs:
        copy.wait()
    for core in range(2):

        @pl.when(apa == core)
        def _():
            ahead, across, stay = sends(core, False)
            for copy in ahead + across:
                copy.wait_send()


def local(
    waveforms,
    time_kernel,
    wire_slot,
    tick_offset,
    bad_channel,
    induction_real,
    induction_imaginary,
    induction_filter,
    collection_real,
    collection_imaginary,
    collection_filter,
):
    channels = wire_slot.shape[0]
    induction, collection = induction_real.shape[1], collection_real.shape[0]
    padded_i, padded_c = rounded_up(induction), rounded_up(collection)
    rows = 2 * padded_i + padded_c
    chunks = channels // CHUNK
    pieces = chunks // 2
    split = (1, channels)
    operands = [
        time_kernel,
        wire_slot.reshape(split),
        tick_offset.reshape(split),
        bad_channel.reshape(split),
        induction_real,
        induction_imaginary,
        induction_filter,
        collection_real.reshape(1, collection),
        collection_imaginary.reshape(1, collection),
        collection_filter.reshape(1, collection),
        *phase_tables(induction),
        *phase_tables(collection),
    ]
    far = pl.BlockSpec(memory_space=pltpu.HBM)
    return pl.pallas_call(
        functools.partial(kernel, induction, collection),
        out_shape=jax.ShapeDtypeStruct((channels, LANES), jnp.float32),
        in_specs=[far] * (1 + len(operands)),
        out_specs=far,
        scratch_shapes=[pltpu.VMEM(operand.shape, operand.dtype) for operand in operands]
        + [
            pltpu.VMEM((chunks, CHUNK, LANES), jnp.bfloat16),
            pltpu.VMEM((chunks, CHUNK, LANES), jnp.bfloat16),
            pltpu.VMEM((pieces, rows, 2 * CHUNK), jnp.bfloat16),
            pltpu.VMEM((rows, 2 * LANES), jnp.float32),
            pltpu.VMEM((padded_i, padded_i), jnp.bfloat16),
            pltpu.VMEM((padded_i, padded_i), jnp.bfloat16),
            pltpu.VMEM((padded_c, padded_c), jnp.bfloat16),
            pltpu.VMEM((8, 8 * LANES), jnp.float32),
            pltpu.VMEM((32, 2 * LANES), jnp.float32),
            pltpu.VMEM((8, 2 * max(padded_i, padded_c)), jnp.float32),
            pltpu.VMEM((8, LANES), jnp.float32),
            pltpu.VMEM((channels, LANES), jnp.float32),
            pltpu.SemaphoreType.DMA((pieces,)),
            pltpu.SemaphoreType.DMA((pieces,)),
            pltpu.SemaphoreType.DMA((pieces,)),
            pltpu.SemaphoreType.DMA((chunks,)),
            pltpu.SemaphoreType.DMA((chunks,)),
            pltpu.SemaphoreType.DMA((len(operands),)),
            pltpu.SemaphoreType.DMA((3,)),
        ],
        compiler_params=pltpu.CompilerParams(
            collective_id=0, has_side_effects=True, vmem_limit_bytes=62 * 1024 * 1024
        ),
    )(waveforms, *operands)


def solution(mesh):
    placed = (
        P(("grp", "apa"), "tm"),
        P(),
        P("grp"),
        P("grp"),
        P("grp"),
        P(),
        P(),
        P(),
        P(),
        P(),
        P(),
    )
    return jax.shard_map(
        local, mesh=mesh, in_specs=placed, out_specs=P("grp", ("tm", "apa")), check_vma=False
    )
```

```python
import functools
import math

import jax
import jax.numpy as jnp
import numpy as np
from jax import lax
from jax.experimental import pallas as pl
from jax.experimental.pallas import tpu as pltpu
from jax.sharding import PartitionSpec as P

LANES = 128
CHUNK = 128
MESH = pl.DeviceIdType.MESH


def rounded_up(count):
    return -(-count // LANES) * LANES


def phase_tables(wire_count):
    padded = rounded_up(wire_count)
    columns = (padded - np.arange(padded)) % wire_count

    def both(multiples):
        angle = (multiples[:, None] * columns[None, :] % wire_count) * (2.0 * math.pi / wire_count)
        return np.concatenate([np.cos(angle), np.sin(angle)], 0)

    fine, coarse = both(np.arange(LANES)), both(LANES * np.arange(8))
    return fine.astype(np.float32), coarse.astype(np.float32)


def halves(values):
    high = values.astype(jnp.bfloat16)
    return high, (values - high.astype(jnp.float32)).astype(jnp.bfloat16)


def strided(row):
    return pltpu.roll(jnp.broadcast_to(row, (LANES, LANES)), 0, 1, stride=1, stride_axis=0)


def kernel(induction, collection, waves, *refs):
    operands, out, copies = refs[:14], refs[14], refs[15:29]
    (
        halo,
        main,
        onehot,
        total,
        circulant_u,
        circulant_v,
        circulant_w,
        spread,
        folded,
        rows_h,
        kernel_rows,
        toeplitz,
        result,
        next_send,
        near_send,
        far_send,
        halo_sem,
        main_sem,
        fetch_sem,
        out_sem,
    ) = refs[29:]
    (
        taps,
        slots,
        offsets,
        bad,
        induction_real,
        induction_imaginary,
        induction_filter,
        collection_real,
        collection_imaginary,
        collection_filter,
        fine_uv,
        coarse_uv,
        fine_w,
        coarse_w,
    ) = copies
    tm, apa = lax.axis_index("tm"), lax.axis_index("apa")
    windows = lax.axis_size("tm")
    following = lax.rem(tm + 1, windows)
    previous = lax.rem(tm + windows - 1, windows)
    pieces = waves.shape[0] // CHUNK
    sizes = (induction, induction, collection)
    starts = (0, induction, 2 * induction)

    barrier = pltpu.get_barrier_semaphore()

    def greet(window, core):
        pl.semaphore_signal(
            barrier, inc=1, device_id={"tm": window, "apa": core}, device_id_type=MESH
        )

    greet(tm, 1 - apa)

    @pl.when(apa == 0)
    def _():
        greet(previous, 0)
        greet(previous, 1)

    fetches = [
        pltpu.make_async_copy(source, copy, fetch_sem.at[number])
        for number, (source, copy) in enumerate(zip(operands, copies))
    ]
    for fetch in fetches[:10]:
        fetch.start()
    pl.semaphore_wait(barrier, 2)

    def part(index, half):
        return waves.at[pl.ds(index * CHUNK, CHUNK), pl.ds(half * LANES, LANES)]

    def push(index, half, target, arrived, sent, window, core):
        return pltpu.make_async_remote_copy(
            src_ref=part(index, half),
            dst_ref=target,
            send_sem=sent,
            recv_sem=arrived,
            device_id={"tm": window, "apa": core},
            device_id_type=MESH,
        )

    def sends(core, kept=True):
        first = core * pieces
        ahead = [
            push(k, 1, halo.at[first + k], halo_sem.at[first + k], next_send.at[k], following, 0)
            for k in range(pieces)
        ]
        across, stay = [], []
        for k in range(pieces):
            spot = first + k
            if core == 0:
                across.append(
                    push(k, 0, halo.at[spot], halo_sem.at[spot], near_send.at[k], tm, 1)
                )
                across.append(
                    push(k, 1, main.at[spot], main_sem.at[spot], far_send.at[k], tm, 1)
                )
                kept and stay.append(pltpu.make_async_copy(part(k, 0), main.at[spot], main_sem.at[spot]))
            else:
                across.append(
                    push(k, 0, main.at[spot], main_sem.at[spot], near_send.at[k], tm, 0)
                )
                kept and stay.append(pltpu.make_async_copy(part(k, 0), halo.at[spot], halo_sem.at[spot]))
                kept and stay.append(pltpu.make_async_copy(part(k, 1), main.at[spot], main_sem.at[spot]))
        return ahead, across, stay

    for core in range(2):

        @pl.when(apa == core)
        def _():
            ahead, across, stay = sends(core)
            for copy in ahead + across + stay:
                copy.start()

    for fetch in fetches[10:]:
        fetch.start()
    for fetch in fetches[:10]:
        fetch.wait()

    build_rows = math.gcd(total.shape[0], 256)
    counted = lax.broadcasted_iota(jnp.int32, (build_rows, 2 * CHUNK), 0).astype(jnp.int16)
    one, zero = jnp.bfloat16(1), jnp.bfloat16(0)

    def span_of(ref, first, count):
        return ref[pl.ds(pl.multiple_of(first, LANES), count)].reshape(1, count)

    def joined(ref, step):
        return jnp.concatenate(
            [span_of(ref, index * CHUNK, CHUNK) for index in (step, pieces + step)], 1
        )

    def make_onehot(step, carry):
        slot = joined(slots, step)
        slot = jnp.where(joined(bad, step) == 0, slot, -1)
        for start in range(0, total.shape[0], build_rows):
            hit = counted == (slot - start).astype(jnp.int16)
            onehot[step, start : start + build_rows, :] = jnp.where(hit, one, zero)
        return carry

    lax.fori_loop(0, pieces, make_onehot, 0)
    total[...] = jnp.zeros_like(total)

    spread[...] = jnp.zeros_like(spread)
    kernel_rows[...] = jnp.zeros_like(kernel_rows)
    kernel_rows[0:3, 0 : taps.shape[1]] = taps[...].astype(jnp.float32)
    for real, imaginary, gain, row in (
        (induction_real, induction_imaginary, induction_filter, 0),
        (collection_real, collection_imaginary, collection_filter, 4),
    ):
        count, width = real.shape
        re, im = real[...], imaginary[...]
        magnitude = re * re + im * im
        spread[row : row + count, 0:width] = gain[...] * re / magnitude
        spread[row + count : row + 2 * count, 0:width] = -gain[...] * im / magnitude
    for fetch in fetches[10:]:
        fetch.wait()
    lane = lax.broadcasted_iota(jnp.int32, (LANES, LANES), 1)
    row_of = lax.broadcasted_iota(jnp.int32, (LANES, LANES), 0)
    for fine, coarse, count, first, targets, wires in (
        (fine_uv, coarse_uv, 2, 0, (circulant_u, circulant_v), induction),
        (fine_w, coarse_w, 1, 4, (circulant_w,), collection),
    ):
        padded = rounded_up(wires)
        blocks = padded // LANES
        for entry in range(count):
            for block in range(8):
                columns = slice(block * LANES, (block + 1) * LANES)
                re = spread[first + entry : first + entry + 1, columns]
                im = spread[first + count + entry : first + count + entry + 1, columns]
                row = 16 * entry + block
                folded[row : row + 1, 0:LANES] = re
                folded[row : row + 1, LANES : 2 * LANES] = -im
                folded[row + 8 : row + 9, 0:LANES] = im
                folded[row + 8 : row + 9, LANES : 2 * LANES] = re
        both = jnp.concatenate(halves(folded[0 : 16 * count, :]), 0)
        terms = sum(
            jnp.dot(both, table, preferred_element_type=jnp.float32) for table in halves(fine[...])
        )
        terms = terms[: 16 * count] + terms[16 * count :]
        for entry in range(count):
            re = terms[16 * entry : 16 * entry + 8]
            im = terms[16 * entry + 8 : 16 * entry + 16]
            turned = coarse[0:8, :] * re - coarse[8:16, :] * im
            line = jnp.sum(turned, axis=0, keepdims=True) * (1.0 / wires)
            rows_h[0:1, 0:padded] = line
            rows_h[0:1, wires : wires + padded] = line
            if padded > wires:
                rows_h[0:1, 2 * wires : 2 * padded] = line[:, : 2 * (padded - wires)]
            before = strided(rows_h[0:1, 0:LANES])
            for k in range(2 * blocks - 1):
                after = strided(rows_h[0:1, (k + 1) * LANES : (k + 2) * LANES])
                piece = jnp.where(lane >= row_of, after, before).astype(jnp.bfloat16)
                for i in range(targets[entry].shape[0] // LANES):
                    j = k - (blocks - 1) + i
                    if 0 <= j < blocks:
                        targets[entry][
                            i * LANES : (i + 1) * LANES, j * LANES : (j + 1) * LANES
                        ] = piece
                before = after

    for plane in range(3):
        turned = strided(kernel_rows[plane : plane + 1, :])
        columns = slice(plane * LANES, (plane + 1) * LANES)
        toeplitz[0:LANES, columns] = jnp.where(lane < row_of, turned, 0.0).astype(jnp.bfloat16)
        toeplitz[LANES : 2 * LANES, columns] = jnp.where(lane >= row_of, turned, 0.0).astype(
            jnp.bfloat16
        )

    def take(step, carry):
        groups = []
        for index in (step, pieces + step):
            pltpu.make_async_copy(main.at[index], main.at[index], main_sem.at[index]).wait()
            pltpu.make_async_copy(halo.at[index], halo.at[index], halo_sem.at[index]).wait()
        for index in (step, pieces + step):
            for start in range(0, CHUNK, LANES):
                delay = span_of(offsets, index * CHUNK + start, LANES).astype(jnp.float32)
                delay = jnp.broadcast_to(delay, (LANES, LANES)).T.astype(jnp.int32)
                origin = (lane - delay) & (LANES - 1)
                early = halo[index, start : start + LANES, :].astype(jnp.float32)
                late = main[index, start : start + LANES, :].astype(jnp.float32)
                early = jnp.take_along_axis(early, origin, axis=1)
                late = jnp.take_along_axis(late, origin, axis=1)
                late = jnp.where(lane >= delay, late, early)
                groups.append(jnp.concatenate([early, late], 1).astype(jnp.bfloat16))
        aligned = jnp.concatenate(groups, 0)
        filtered = jnp.dot(aligned, toeplitz[...], preferred_element_type=jnp.float32).astype(
            jnp.bfloat16
        )
        for plane, (start, wires) in enumerate(zip(starts, sizes)):
            total[start : start + wires, :] += jnp.dot(
                onehot[step, start : start + wires, :],
                filtered[:, plane * LANES : (plane + 1) * LANES],
                preferred_element_type=jnp.float32,
            )
        return carry

    lax.fori_loop(0, pieces, take, 0)

    outs = []
    for plane, circulant in enumerate((circulant_u, circulant_v, circulant_w)):
        start, wires = starts[plane], sizes[plane]
        half, spare = wires // 2, rounded_up(wires) - wires
        top = total[start : start + half, :].astype(jnp.bfloat16)
        bottom = total[start + half : start + wires, :].astype(jnp.bfloat16)
        stacked = [jnp.concatenate([top, bottom], 1), jnp.concatenate([bottom, top], 1)]
        if spare:
            stacked.append(jnp.zeros((spare, 2 * LANES), jnp.bfloat16))
        values = jnp.dot(
            circulant[0:half, :],
            jnp.concatenate(stacked, 0),
            preferred_element_type=jnp.float32,
        )
        result[start : start + half, :] = values[:, 0:LANES]
        result[start + half : start + wires, :] = values[:, LANES:]
        span = pl.ds(start, wires)
        outs.append(pltpu.make_async_copy(result.at[span], out.at[span], out_sem.at[plane]))
        outs[-1].start()
    for copy in outs:
        copy.wait()
    for core in range(2):

        @pl.when(apa == core)
        def _():
            ahead, across, stay = sends(core, False)
            for copy in ahead + across:
                copy.wait_send()


def hand_over(found, out, sems):
    pieces = sems.shape[0]
    rows = found.shape[0] // pieces
    copies = [
        pltpu.make_async_copy(
            found.at[pl.ds(k * rows, rows)], out.at[pl.ds(k * rows, rows)], sems.at[k]
        )
        for k in range(pieces)
    ]
    for copy in copies:
        copy.start()
    for copy in copies:
        copy.wait()


def local(
    waveforms,
    time_kernel,
    wire_slot,
    tick_offset,
    bad_channel,
    induction_real,
    induction_imaginary,
    induction_filter,
    collection_real,
    collection_imaginary,
    collection_filter,
):
    channels = wire_slot.shape[0]
    induction, collection = induction_real.shape[1], collection_real.shape[0]
    padded_i, padded_c = rounded_up(induction), rounded_up(collection)
    half_i, half_c = rounded_up(induction // 2), rounded_up(collection // 2)
    chunks = channels // CHUNK
    pieces = chunks // 2
    operands = [
        time_kernel,
        wire_slot,
        tick_offset,
        bad_channel,
        induction_real,
        induction_imaginary,
        induction_filter,
        collection_real.reshape(1, collection),
        collection_imaginary.reshape(1, collection),
        collection_filter.reshape(1, collection),
        *phase_tables(induction),
        *phase_tables(collection),
    ]
    far = pl.BlockSpec(memory_space=pltpu.HBM)
    found = pl.pallas_call(
        functools.partial(kernel, induction, collection),
        out_shape=jax.ShapeDtypeStruct((channels, LANES), jnp.float32),
        in_specs=[far] * (1 + len(operands)),
        out_specs=far,
        scratch_shapes=[pltpu.VMEM(operand.shape, operand.dtype) for operand in operands]
        + [
            pltpu.VMEM((chunks, CHUNK, LANES), jnp.bfloat16),
            pltpu.VMEM((chunks, CHUNK, LANES), jnp.bfloat16),
            pltpu.VMEM((pieces, channels, 2 * CHUNK), jnp.bfloat16),
            pltpu.VMEM((channels, LANES), jnp.float32),
            pltpu.VMEM((half_i, padded_i), jnp.bfloat16),
            pltpu.VMEM((half_i, padded_i), jnp.bfloat16),
            pltpu.VMEM((half_c, padded_c), jnp.bfloat16),
            pltpu.VMEM((8, 8 * LANES), jnp.float32),
            pltpu.VMEM((32, 2 * LANES), jnp.float32),
            pltpu.VMEM((8, 2 * max(padded_i, padded_c)), jnp.float32),
            pltpu.VMEM((8, LANES), jnp.float32),
            pltpu.VMEM((2 * LANES, 3 * LANES), jnp.bfloat16),
            pltpu.VMEM((channels, LANES), jnp.float32),
            pltpu.SemaphoreType.DMA((pieces,)),
            pltpu.SemaphoreType.DMA((pieces,)),
            pltpu.SemaphoreType.DMA((pieces,)),
            pltpu.SemaphoreType.DMA((chunks,)),
            pltpu.SemaphoreType.DMA((chunks,)),
            pltpu.SemaphoreType.DMA((len(operands),)),
            pltpu.SemaphoreType.DMA((3,)),
        ],
        compiler_params=pltpu.CompilerParams(
            collective_id=0, has_side_effects=True, vmem_limit_bytes=62 * 1024 * 1024
        ),
    )(waveforms, *operands)
    return pl.pallas_call(
        hand_over,
        out_shape=jax.ShapeDtypeStruct(found.shape, found.dtype),
        in_specs=[far],
        out_specs=far,
        scratch_shapes=[pltpu.SemaphoreType.DMA((8,))],
        compiler_params=pltpu.CompilerParams(vmem_limit_bytes=62 * 1024 * 1024),
    )(found)


def solution(mesh):
    placed = (
        P(("grp", "apa"), "tm"),
        P(),
        P("grp"),
        P("grp"),
        P("grp"),
        P(),
        P(),
        P(),
        P(),
        P(),
        P(),
    )
    return jax.shard_map(
        local, mesh=mesh, in_specs=placed, out_specs=P("grp", ("tm", "apa")), check_vma=False
    )
```

```python
import functools
import math

import jax
import jax.numpy as jnp
import numpy as np
from jax import lax
from jax.experimental import pallas as pl
from jax.experimental.pallas import tpu as pltpu
from jax.sharding import PartitionSpec as P

LANES = 128
CHUNK = 256
MESH = pl.DeviceIdType.MESH


def rounded_up(count):
    return -(-count // LANES) * LANES


def phase_tables(wire_count):
    padded = rounded_up(wire_count)
    columns = (padded - np.arange(padded)) % wire_count

    def both(multiples):
        angle = (multiples[:, None] * columns[None, :] % wire_count) * (2.0 * math.pi / wire_count)
        return np.concatenate([np.cos(angle), np.sin(angle)], 0)

    fine, coarse = both(np.arange(LANES)), both(LANES * np.arange(8))
    return fine.astype(np.float32), coarse.astype(np.float32)


def halves(values):
    high = values.astype(jnp.bfloat16)
    return high, (values - high.astype(jnp.float32)).astype(jnp.bfloat16)


def strided(row):
    return pltpu.roll(jnp.broadcast_to(row, (LANES, LANES)), 0, 1, stride=1, stride_axis=0)


def kernel(induction, collection, waves, *refs):
    operands, out, copies = refs[:14], refs[14], refs[15:29]
    (
        halo,
        main,
        staged,
        origins,
        total,
        circulant_u,
        circulant_v,
        circulant_w,
        spread,
        folded,
        rows_h,
        kernel_rows,
        toeplitz,
        result,
        next_send,
        near_send,
        far_send,
        halo_sem,
        main_sem,
        own_sem,
        fetch_sem,
        out_sem,
    ) = refs[29:]
    (
        taps,
        slots,
        offsets,
        bad,
        induction_real,
        induction_imaginary,
        induction_filter,
        collection_real,
        collection_imaginary,
        collection_filter,
        fine_uv,
        coarse_uv,
        fine_w,
        coarse_w,
    ) = copies
    tm, apa = lax.axis_index("tm"), lax.axis_index("apa")
    windows = lax.axis_size("tm")
    following = lax.rem(tm + 1, windows)
    previous = lax.rem(tm + windows - 1, windows)
    pieces = waves.shape[0] // CHUNK
    sizes = (induction, induction, collection)
    starts = (0, induction, 2 * induction)

    barrier = pltpu.get_barrier_semaphore()

    def greet(window, core):
        pl.semaphore_signal(
            barrier, inc=1, device_id={"tm": window, "apa": core}, device_id_type=MESH
        )

    greet(tm, 1 - apa)

    @pl.when(apa == 0)
    def _():
        greet(previous, 0)
        greet(previous, 1)

    fetches = [
        pltpu.make_async_copy(source, copy, fetch_sem.at[number])
        for number, (source, copy) in enumerate(zip(operands, copies))
    ]
    def own_halves(core):
        copies = ([], [])
        for k in range(pieces):
            spot = core * pieces + k
            targets = (halo.at[spot], main.at[spot]) if core else (main.at[spot], staged.at[k])
            for half in range(2):
                source = waves.at[pl.ds(k * CHUNK, CHUNK), pl.ds(half * LANES, LANES)]
                copies[half].append(
                    pltpu.make_async_copy(source, targets[half], own_sem.at[half, k])
                )
        return copies

    for core in range(2):

        @pl.when(apa == core)
        def _():
            firsts, seconds = own_halves(core)
            for copy in seconds + firsts:
                copy.start()

    for fetch in fetches[:10]:
        fetch.start()
    pl.semaphore_wait(barrier, 2)

    def push(source, target, arrived, sent, window, core):
        return pltpu.make_async_remote_copy(
            src_ref=source,
            dst_ref=target,
            send_sem=sent,
            recv_sem=arrived,
            device_id={"tm": window, "apa": core},
            device_id_type=MESH,
        )

    def sends(core):
        ahead, across = [], []
        for k in range(pieces):
            spot = core * pieces + k
            second = main.at[spot] if core else staged.at[k]
            ahead.append(
                push(second, halo.at[spot], halo_sem.at[spot], next_send.at[k], following, 0)
            )
            if core == 0:
                across.append(
                    push(main.at[spot], halo.at[spot], halo_sem.at[spot], near_send.at[k], tm, 1)
                )
                across.append(
                    push(second, main.at[spot], main_sem.at[spot], far_send.at[k], tm, 1)
                )
            else:
                across.append(
                    push(halo.at[spot], main.at[spot], main_sem.at[spot], near_send.at[k], tm, 0)
                )
        return ahead, across

    for core in range(2):

        @pl.when(apa == core)
        def _():
            ahead, across = sends(core)
            firsts, seconds = own_halves(core)
            for copy, send in zip(seconds, ahead):
                copy.wait()
                send.start()
            for copy in firsts:
                copy.wait()
            for send in across:
                send.start()

    for fetch in fetches[10:]:
        fetch.start()
    for fetch in fetches[:10]:
        fetch.wait()

    build_rows = math.gcd(induction, collection)
    counted = lax.broadcasted_iota(jnp.int32, (build_rows, 2 * CHUNK), 0).astype(jnp.int16)
    one, zero = jnp.bfloat16(1), jnp.bfloat16(0)
    lane = lax.broadcasted_iota(jnp.int32, (LANES, LANES), 1)
    row_of = lax.broadcasted_iota(jnp.int32, (LANES, LANES), 0)

    def span_of(ref, first, count):
        return ref[pl.ds(pl.multiple_of(first, LANES), count)].reshape(1, count)

    def joined(ref, step):
        return jnp.concatenate(
            [span_of(ref, index * CHUNK, CHUNK) for index in (step, pieces + step)], 1
        )

    def plane_rows(slot, start, wires):
        hits = [
            jnp.where(counted == (slot - first).astype(jnp.int16), one, zero)
            for first in range(start, start + wires, build_rows)
        ]
        return jnp.concatenate(hits, 0)

    def make_origins(group, carry):
        first = pl.multiple_of(group * LANES, LANES)
        delay = span_of(offsets, first, LANES).astype(jnp.float32)
        delay = jnp.broadcast_to(delay, (LANES, LANES)).T.astype(jnp.int32)
        origins[pl.ds(first, LANES), :] = (lane - delay) & (LANES - 1)
        return carry

    lax.fori_loop(0, origins.shape[0] // LANES, make_origins, 0)
    total[...] = jnp.zeros_like(total)

    spread[...] = jnp.zeros_like(spread)
    kernel_rows[...] = jnp.zeros_like(kernel_rows)
    kernel_rows[0:3, 0 : taps.shape[1]] = taps[...].astype(jnp.float32)
    for real, imaginary, gain, row in (
        (induction_real, induction_imaginary, induction_filter, 0),
        (collection_real, collection_imaginary, collection_filter, 4),
    ):
        count, width = real.shape
        re, im = real[...], imaginary[...]
        magnitude = re * re + im * im
        spread[row : row + count, 0:width] = gain[...] * re / magnitude
        spread[row + count : row + 2 * count, 0:width] = -gain[...] * im / magnitude
    for fetch in fetches[10:]:
        fetch.wait()
    for fine, coarse, count, first, targets, wires in (
        (fine_uv, coarse_uv, 2, 0, (circulant_u, circulant_v), induction),
        (fine_w, coarse_w, 1, 4, (circulant_w,), collection),
    ):
        padded = rounded_up(wires)
        blocks = padded // LANES
        for entry in range(count):
            for block in range(8):
                columns = slice(block * LANES, (block + 1) * LANES)
                re = spread[first + entry : first + entry + 1, columns]
                im = spread[first + count + entry : first + count + entry + 1, columns]
                row = 16 * entry + block
                folded[row : row + 1, 0:LANES] = re
                folded[row : row + 1, LANES : 2 * LANES] = -im
                folded[row + 8 : row + 9, 0:LANES] = im
                folded[row + 8 : row + 9, LANES : 2 * LANES] = re
        both = jnp.concatenate(halves(folded[0 : 16 * count, :]), 0)
        terms = sum(
            jnp.dot(both, table, preferred_element_type=jnp.float32) for table in halves(fine[...])
        )
        terms = terms[: 16 * count] + terms[16 * count :]
        for entry in range(count):
            re = terms[16 * entry : 16 * entry + 8]
            im = terms[16 * entry + 8 : 16 * entry + 16]
            turned = coarse[0:8, :] * re - coarse[8:16, :] * im
            line = jnp.sum(turned, axis=0, keepdims=True) * (1.0 / wires)
            rows_h[0:1, 0:padded] = line
            rows_h[0:1, wires : wires + padded] = line
            if padded > wires:
                rows_h[0:1, 2 * wires : 2 * padded] = line[:, : 2 * (padded - wires)]
            before = strided(rows_h[0:1, 0:LANES])
            for k in range(2 * blocks - 1):
                after = strided(rows_h[0:1, (k + 1) * LANES : (k + 2) * LANES])
                piece = jnp.where(lane >= row_of, after, before).astype(jnp.bfloat16)
                for i in range(targets[entry].shape[0] // LANES):
                    j = k - (blocks - 1) + i
                    if 0 <= j < blocks:
                        targets[entry][
                            i * LANES : (i + 1) * LANES, j * LANES : (j + 1) * LANES
                        ] = piece
                before = after

    for plane in range(3):
        turned = strided(kernel_rows[plane : plane + 1, :])
        columns = slice(plane * LANES, (plane + 1) * LANES)
        toeplitz[0:LANES, columns] = jnp.where(lane < row_of, turned, 0.0).astype(jnp.bfloat16)
        toeplitz[LANES : 2 * LANES, columns] = jnp.where(lane >= row_of, turned, 0.0).astype(
            jnp.bfloat16
        )

    def take(step, carry):
        groups = []
        for half in range(2):
            index = half * pieces + step

            @pl.when(apa != half)
            def _():
                pltpu.make_async_copy(main.at[index], main.at[index], main_sem.at[index]).wait()

            @pl.when(apa * half == 0)
            def _():
                pltpu.make_async_copy(halo.at[index], halo.at[index], halo_sem.at[index]).wait()

        for index in (step, pieces + step):
            for start in range(0, CHUNK, LANES):
                origin = origins[
                    pl.ds(pl.multiple_of(index * CHUNK + start, LANES), LANES), :
                ]
                early = halo[index, start : start + LANES, :].astype(jnp.float32)
                late = main[index, start : start + LANES, :].astype(jnp.float32)
                early = jnp.take_along_axis(early, origin, axis=1)
                late = jnp.take_along_axis(late, origin, axis=1)
                late = jnp.where(lane >= origin, late, early)
                groups.append(jnp.concatenate([early, late], 1).astype(jnp.bfloat16))
        slot = jnp.where(joined(bad, step) == 0, joined(slots, step), -1)
        aligned = jnp.concatenate(groups, 0)
        filtered = jnp.dot(aligned, toeplitz[...], preferred_element_type=jnp.float32).astype(
            jnp.bfloat16
        )
        for plane, (start, wires) in enumerate(zip(starts, sizes)):
            total[start : start + wires, :] += jnp.dot(
                plane_rows(slot, start, wires),
                filtered[:, plane * LANES : (plane + 1) * LANES],
                preferred_element_type=jnp.float32,
            )
        return carry

    lax.fori_loop(0, pieces, take, 0)

    outs = []
    for plane, circulant in enumerate((circulant_u, circulant_v, circulant_w)):
        start, wires = starts[plane], sizes[plane]
        half, spare = wires // 2, rounded_up(wires) - wires
        top = total[start : start + half, :].astype(jnp.bfloat16)
        bottom = total[start + half : start + wires, :].astype(jnp.bfloat16)
        stacked = [jnp.concatenate([top, bottom], 1), jnp.concatenate([bottom, top], 1)]
        if spare:
            stacked.append(jnp.zeros((spare, 2 * LANES), jnp.bfloat16))
        values = jnp.dot(
            circulant[0:half, :],
            jnp.concatenate(stacked, 0),
            preferred_element_type=jnp.float32,
        )
        result[start : start + half, :] = values[:, 0:LANES]
        result[start + half : start + wires, :] = values[:, LANES:]
        span = pl.ds(start, wires)
        outs.append(pltpu.make_async_copy(result.at[span], out.at[span], out_sem.at[plane]))
        outs[-1].start()
    for copy in outs:
        copy.wait()
    for core in range(2):

        @pl.when(apa == core)
        def _():
            ahead, across = sends(core)
            for copy in ahead + across:
                copy.wait_send()


def hand_over(found, out, held, arrive, leave):
    pieces = arrive.shape[0]
    rows = found.shape[0] // pieces
    spans = [pl.ds(k * rows, rows) for k in range(pieces)]
    inward = [
        pltpu.make_async_copy(found.at[span], held.at[span], arrive.at[k])
        for k, span in enumerate(spans)
    ]
    outward = [
        pltpu.make_async_copy(held.at[span], out.at[span], leave.at[k])
        for k, span in enumerate(spans)
    ]
    for copy in inward:
        copy.start()
    for copy, after in zip(inward, outward):
        copy.wait()
        after.start()
    for copy in outward:
        copy.wait()


def local(
    waveforms,
    time_kernel,
    wire_slot,
    tick_offset,
    bad_channel,
    induction_real,
    induction_imaginary,
    induction_filter,
    collection_real,
    collection_imaginary,
    collection_filter,
):
    channels = wire_slot.shape[0]
    induction, collection = induction_real.shape[1], collection_real.shape[0]
    padded_i, padded_c = rounded_up(induction), rounded_up(collection)
    half_i, half_c = rounded_up(induction // 2), rounded_up(collection // 2)
    chunks = channels // CHUNK
    pieces = chunks // 2
    operands = [
        time_kernel,
        wire_slot,
        tick_offset,
        bad_channel,
        induction_real,
        induction_imaginary,
        induction_filter,
        collection_real.reshape(1, collection),
        collection_imaginary.reshape(1, collection),
        collection_filter.reshape(1, collection),
        *phase_tables(induction),
        *phase_tables(collection),
    ]
    far = pl.BlockSpec(memory_space=pltpu.HBM)
    found = pl.pallas_call(
        functools.partial(kernel, induction, collection),
        out_shape=jax.ShapeDtypeStruct((channels, LANES), jnp.float32),
        in_specs=[far] * (1 + len(operands)),
        out_specs=far,
        scratch_shapes=[pltpu.VMEM(operand.shape, operand.dtype) for operand in operands]
        + [
            pltpu.VMEM((chunks, CHUNK, LANES), jnp.bfloat16),
            pltpu.VMEM((chunks, CHUNK, LANES), jnp.bfloat16),
            pltpu.VMEM((pieces, CHUNK, LANES), jnp.bfloat16),
            pltpu.VMEM((channels, LANES), jnp.int32),
            pltpu.VMEM((channels, LANES), jnp.float32),
            pltpu.VMEM((half_i, padded_i), jnp.bfloat16),
            pltpu.VMEM((half_i, padded_i), jnp.bfloat16),
            pltpu.VMEM((half_c, padded_c), jnp.bfloat16),
            pltpu.VMEM((8, 8 * LANES), jnp.float32),
            pltpu.VMEM((32, 2 * LANES), jnp.float32),
            pltpu.VMEM((8, 2 * max(padded_i, padded_c)), jnp.float32),
            pltpu.VMEM((8, LANES), jnp.float32),
            pltpu.VMEM((2 * LANES, 3 * LANES), jnp.bfloat16),
            pltpu.VMEM((channels, LANES), jnp.float32),
            pltpu.SemaphoreType.DMA((pieces,)),
            pltpu.SemaphoreType.DMA((pieces,)),
            pltpu.SemaphoreType.DMA((pieces,)),
            pltpu.SemaphoreType.DMA((chunks,)),
            pltpu.SemaphoreType.DMA((chunks,)),
            pltpu.SemaphoreType.DMA((2, pieces)),
            pltpu.SemaphoreType.DMA((len(operands),)),
            pltpu.SemaphoreType.DMA((3,)),
        ],
        compiler_params=pltpu.CompilerParams(
            collective_id=0, has_side_effects=True, vmem_limit_bytes=62 * 1024 * 1024
        ),
    )(waveforms, *operands)
    return pl.pallas_call(
        hand_over,
        out_shape=jax.ShapeDtypeStruct(found.shape, found.dtype),
        in_specs=[far],
        out_specs=far,
        scratch_shapes=[pltpu.VMEM(found.shape, found.dtype)]
        + [pltpu.SemaphoreType.DMA((4,)) for _ in range(2)],
        compiler_params=pltpu.CompilerParams(vmem_limit_bytes=62 * 1024 * 1024),
    )(found)


def solution(mesh):
    placed = (
        P(("grp", "apa"), "tm"),
        P(),
        P("grp"),
        P("grp"),
        P("grp"),
        P(),
        P(),
        P(),
        P(),
        P(),
        P(),
    )
    return jax.shard_map(
        local, mesh=mesh, in_specs=placed, out_specs=P("grp", ("tm", "apa")), check_vma=False
    )
```

```python
import functools
import math

import jax
import jax.numpy as jnp
import numpy as np
from jax import lax
from jax.experimental import pallas as pl
from jax.experimental.pallas import tpu as pltpu
from jax.sharding import PartitionSpec as P

LANES = 128
CHUNK = 256
MESH = pl.DeviceIdType.MESH


def rounded_up(count):
    return -(-count // LANES) * LANES


def phase_tables(wire_count):
    padded = rounded_up(wire_count)
    columns = (padded - np.arange(padded)) % wire_count

    def both(multiples):
        angle = (multiples[:, None] * columns[None, :] % wire_count) * (2.0 * math.pi / wire_count)
        return np.concatenate([np.cos(angle), np.sin(angle)], 0)

    fine, coarse = both(np.arange(LANES)), both(LANES * np.arange(8))
    return fine.astype(np.float32), coarse.astype(np.float32)


def halves(values):
    high = values.astype(jnp.bfloat16)
    return high, (values - high.astype(jnp.float32)).astype(jnp.bfloat16)


def strided(row):
    return pltpu.roll(jnp.broadcast_to(row, (LANES, LANES)), 0, 1, stride=1, stride_axis=0)


def kernel(induction, collection, waves, *refs):
    operands, out, copies = refs[:14], refs[14], refs[15:29]
    (
        halo,
        main,
        staged,
        origins,
        total,
        circulant_u,
        circulant_v,
        circulant_w,
        spread,
        folded,
        rows_h,
        kernel_rows,
        toeplitz,
        next_send,
        near_send,
        far_send,
        halo_sem,
        main_sem,
        own_sem,
        fetch_sem,
    ) = refs[29:]
    (
        taps,
        slots,
        offsets,
        bad,
        induction_real,
        induction_imaginary,
        induction_filter,
        collection_real,
        collection_imaginary,
        collection_filter,
        fine_uv,
        coarse_uv,
        fine_w,
        coarse_w,
    ) = copies
    tm, apa = lax.axis_index("tm"), lax.axis_index("apa")
    windows = lax.axis_size("tm")
    following = lax.rem(tm + 1, windows)
    previous = lax.rem(tm + windows - 1, windows)
    pieces = waves.shape[0] // CHUNK
    sizes = (induction, induction, collection)
    starts = (0, induction, 2 * induction)

    barrier = pltpu.get_barrier_semaphore()

    def greet(window, core):
        pl.semaphore_signal(
            barrier, inc=1, device_id={"tm": window, "apa": core}, device_id_type=MESH
        )

    greet(tm, 1 - apa)

    @pl.when(apa == 0)
    def _():
        greet(previous, 0)
        greet(previous, 1)

    fetches = [
        pltpu.make_async_copy(source, copy, fetch_sem.at[number])
        for number, (source, copy) in enumerate(zip(operands, copies))
    ]
    def own_halves(core):
        copies = ([], [])
        for k in range(pieces):
            spot = core * pieces + k
            targets = (halo.at[spot], main.at[spot]) if core else (main.at[spot], staged.at[k])
            for half in range(2):
                source = waves.at[pl.ds(k * CHUNK, CHUNK), pl.ds(half * LANES, LANES)]
                copies[half].append(
                    pltpu.make_async_copy(source, targets[half], own_sem.at[half, k])
                )
        return copies

    for core in range(2):

        @pl.when(apa == core)
        def _():
            firsts, seconds = own_halves(core)
            for copy in seconds + firsts:
                copy.start()

    for fetch in fetches[:10]:
        fetch.start()
    pl.semaphore_wait(barrier, 2)

    def push(source, target, arrived, sent, window, core):
        return pltpu.make_async_remote_copy(
            src_ref=source,
            dst_ref=target,
            send_sem=sent,
            recv_sem=arrived,
            device_id={"tm": window, "apa": core},
            device_id_type=MESH,
        )

    def sends(core):
        ahead, across = [], []
        for k in range(pieces):
            spot = core * pieces + k
            second = main.at[spot] if core else staged.at[k]
            ahead.append(
                push(second, halo.at[spot], halo_sem.at[spot], next_send.at[k], following, 0)
            )
            if core == 0:
                across.append(
                    push(main.at[spot], halo.at[spot], halo_sem.at[spot], near_send.at[k], tm, 1)
                )
                across.append(
                    push(second, main.at[spot], main_sem.at[spot], far_send.at[k], tm, 1)
                )
            else:
                across.append(
                    push(halo.at[spot], main.at[spot], main_sem.at[spot], near_send.at[k], tm, 0)
                )
        return ahead, across

    for core in range(2):

        @pl.when(apa == core)
        def _():
            ahead, across = sends(core)
            firsts, seconds = own_halves(core)
            for copy, send in zip(seconds, ahead):
                copy.wait()
                send.start()
            for copy in firsts:
                copy.wait()
            for send in across:
                send.start()

    for fetch in fetches[10:]:
        fetch.start()
    for fetch in fetches[:10]:
        fetch.wait()

    build_rows = math.gcd(induction, collection)
    counted = lax.broadcasted_iota(jnp.int32, (build_rows, 2 * CHUNK), 0).astype(jnp.int16)
    one, zero = jnp.bfloat16(1), jnp.bfloat16(0)
    lane = lax.broadcasted_iota(jnp.int32, (LANES, LANES), 1)
    row_of = lax.broadcasted_iota(jnp.int32, (LANES, LANES), 0)

    def span_of(ref, first, count):
        return ref[pl.ds(pl.multiple_of(first, LANES), count)].reshape(1, count)

    def joined(ref, step):
        return jnp.concatenate(
            [span_of(ref, index * CHUNK, CHUNK) for index in (step, pieces + step)], 1
        )

    def plane_rows(slot, start, wires):
        hits = [
            jnp.where(counted == (slot - first).astype(jnp.int16), one, zero)
            for first in range(start, start + wires, build_rows)
        ]
        return jnp.concatenate(hits, 0)

    def make_origins(group, carry):
        first = pl.multiple_of(group * LANES, LANES)
        delay = span_of(offsets, first, LANES).astype(jnp.float32)
        delay = jnp.broadcast_to(delay, (LANES, LANES)).T.astype(jnp.int32)
        origins[pl.ds(first, LANES), :] = (lane - delay) & (LANES - 1)
        return carry

    lax.fori_loop(0, origins.shape[0] // LANES, make_origins, 0)
    total[...] = jnp.zeros_like(total)

    spread[...] = jnp.zeros_like(spread)
    kernel_rows[...] = jnp.zeros_like(kernel_rows)
    kernel_rows[0:3, 0 : taps.shape[1]] = taps[...].astype(jnp.float32)
    for real, imaginary, gain, row in (
        (induction_real, induction_imaginary, induction_filter, 0),
        (collection_real, collection_imaginary, collection_filter, 4),
    ):
        count, width = real.shape
        re, im = real[...], imaginary[...]
        magnitude = re * re + im * im
        spread[row : row + count, 0:width] = gain[...] * re / magnitude
        spread[row + count : row + 2 * count, 0:width] = -gain[...] * im / magnitude
    for fetch in fetches[10:]:
        fetch.wait()
    for fine, coarse, count, first, targets, wires in (
        (fine_uv, coarse_uv, 2, 0, (circulant_u, circulant_v), induction),
        (fine_w, coarse_w, 1, 4, (circulant_w,), collection),
    ):
        padded = rounded_up(wires)
        blocks = padded // LANES
        for entry in range(count):
            for block in range(8):
                columns = slice(block * LANES, (block + 1) * LANES)
                re = spread[first + entry : first + entry + 1, columns]
                im = spread[first + count + entry : first + count + entry + 1, columns]
                row = 16 * entry + block
                folded[row : row + 1, 0:LANES] = re
                folded[row : row + 1, LANES : 2 * LANES] = -im
                folded[row + 8 : row + 9, 0:LANES] = im
                folded[row + 8 : row + 9, LANES : 2 * LANES] = re
        both = jnp.concatenate(halves(folded[0 : 16 * count, :]), 0)
        terms = sum(
            jnp.dot(both, table, preferred_element_type=jnp.float32) for table in halves(fine[...])
        )
        terms = terms[: 16 * count] + terms[16 * count :]
        for entry in range(count):
            re = terms[16 * entry : 16 * entry + 8]
            im = terms[16 * entry + 8 : 16 * entry + 16]
            turned = coarse[0:8, :] * re - coarse[8:16, :] * im
            line = jnp.sum(turned, axis=0, keepdims=True) * (1.0 / wires)
            rows_h[0:1, 0:padded] = line
            rows_h[0:1, wires : wires + padded] = line
            if padded > wires:
                rows_h[0:1, 2 * wires : 2 * padded] = line[:, : 2 * (padded - wires)]
            before = strided(rows_h[0:1, 0:LANES])
            for k in range(2 * blocks - 1):
                after = strided(rows_h[0:1, (k + 1) * LANES : (k + 2) * LANES])
                piece = jnp.where(lane >= row_of, after, before).astype(jnp.bfloat16)
                for i in range(targets[entry].shape[0] // LANES):
                    j = k - (blocks - 1) + i
                    if 0 <= j < blocks:
                        targets[entry][
                            i * LANES : (i + 1) * LANES, j * LANES : (j + 1) * LANES
                        ] = piece
                before = after

    for plane in range(3):
        turned = strided(kernel_rows[plane : plane + 1, :])
        columns = slice(plane * LANES, (plane + 1) * LANES)
        toeplitz[0:LANES, columns] = jnp.where(lane < row_of, turned, 0.0).astype(jnp.bfloat16)
        toeplitz[LANES : 2 * LANES, columns] = jnp.where(lane >= row_of, turned, 0.0).astype(
            jnp.bfloat16
        )

    def take(step, carry):
        groups = []
        for half in range(2):
            index = half * pieces + step

            @pl.when(apa != half)
            def _():
                pltpu.make_async_copy(main.at[index], main.at[index], main_sem.at[index]).wait()

            @pl.when(apa * half == 0)
            def _():
                pltpu.make_async_copy(halo.at[index], halo.at[index], halo_sem.at[index]).wait()

        for index in (step, pieces + step):
            for start in range(0, CHUNK, LANES):
                origin = origins[
                    pl.ds(pl.multiple_of(index * CHUNK + start, LANES), LANES), :
                ]
                early = halo[index, start : start + LANES, :].astype(jnp.float32)
                late = main[index, start : start + LANES, :].astype(jnp.float32)
                early = jnp.take_along_axis(early, origin, axis=1)
                late = jnp.take_along_axis(late, origin, axis=1)
                late = jnp.where(lane >= origin, late, early)
                groups.append(jnp.concatenate([early, late], 1).astype(jnp.bfloat16))
        slot = jnp.where(joined(bad, step) == 0, joined(slots, step), -1)
        aligned = jnp.concatenate(groups, 0)
        filtered = jnp.dot(aligned, toeplitz[...], preferred_element_type=jnp.float32).astype(
            jnp.bfloat16
        )
        for plane, (start, wires) in enumerate(zip(starts, sizes)):
            total[start : start + wires, :] += jnp.dot(
                plane_rows(slot, start, wires),
                filtered[:, plane * LANES : (plane + 1) * LANES],
                preferred_element_type=jnp.float32,
            )
        return carry

    lax.fori_loop(0, pieces, take, 0)

    for plane, circulant in enumerate((circulant_u, circulant_v, circulant_w)):
        start, wires = starts[plane], sizes[plane]
        half, spare = wires // 2, rounded_up(wires) - wires
        top = total[start : start + half, :].astype(jnp.bfloat16)
        bottom = total[start + half : start + wires, :].astype(jnp.bfloat16)
        stacked = [jnp.concatenate([top, bottom], 1), jnp.concatenate([bottom, top], 1)]
        if spare:
            stacked.append(jnp.zeros((spare, 2 * LANES), jnp.bfloat16))
        values = jnp.dot(
            circulant[0:half, :],
            jnp.concatenate(stacked, 0),
            preferred_element_type=jnp.float32,
        )
        out[start : start + half, :] = values[:, 0:LANES]
        out[start + half : start + wires, :] = values[:, LANES:]
    for core in range(2):

        @pl.when(apa == core)
        def _():
            ahead, across = sends(core)
            for copy in ahead + across:
                copy.wait_send()


def hand_over(found, out, leave):
    pieces = leave.shape[0]
    rows = found.shape[0] // pieces
    copies = [
        pltpu.make_async_copy(
            found.at[pl.ds(k * rows, rows)], out.at[pl.ds(k * rows, rows)], leave.at[k]
        )
        for k in range(pieces)
    ]
    for copy in copies:
        copy.start()
    for copy in copies:
        copy.wait()


def local(
    waveforms,
    time_kernel,
    wire_slot,
    tick_offset,
    bad_channel,
    induction_real,
    induction_imaginary,
    induction_filter,
    collection_real,
    collection_imaginary,
    collection_filter,
):
    channels = wire_slot.shape[0]
    induction, collection = induction_real.shape[1], collection_real.shape[0]
    padded_i, padded_c = rounded_up(induction), rounded_up(collection)
    half_i, half_c = rounded_up(induction // 2), rounded_up(collection // 2)
    chunks = channels // CHUNK
    pieces = chunks // 2
    operands = [
        time_kernel,
        wire_slot,
        tick_offset,
        bad_channel,
        induction_real,
        induction_imaginary,
        induction_filter,
        collection_real.reshape(1, collection),
        collection_imaginary.reshape(1, collection),
        collection_filter.reshape(1, collection),
        *map(jnp.asarray, phase_tables(induction) + phase_tables(collection)),
    ]
    far = pl.BlockSpec(memory_space=pltpu.HBM)
    near = pl.BlockSpec(memory_space=pltpu.VMEM)
    operands = [pltpu.with_memory_space_constraint(operand, pltpu.HBM) for operand in operands]
    found = pl.pallas_call(
        functools.partial(kernel, induction, collection),
        out_shape=pltpu.VMEM((channels, LANES), jnp.float32),
        in_specs=[far] * (1 + len(operands)),
        out_specs=near,
        scratch_shapes=[pltpu.VMEM(operand.shape, operand.dtype) for operand in operands]
        + [
            pltpu.VMEM((chunks, CHUNK, LANES), jnp.bfloat16),
            pltpu.VMEM((chunks, CHUNK, LANES), jnp.bfloat16),
            pltpu.VMEM((pieces, CHUNK, LANES), jnp.bfloat16),
            pltpu.VMEM((channels, LANES), jnp.int32),
            pltpu.VMEM((channels, LANES), jnp.float32),
            pltpu.VMEM((half_i, padded_i), jnp.bfloat16),
            pltpu.VMEM((half_i, padded_i), jnp.bfloat16),
            pltpu.VMEM((half_c, padded_c), jnp.bfloat16),
            pltpu.VMEM((8, 8 * LANES), jnp.float32),
            pltpu.VMEM((32, 2 * LANES), jnp.float32),
            pltpu.VMEM((8, 2 * max(padded_i, padded_c)), jnp.float32),
            pltpu.VMEM((8, LANES), jnp.float32),
            pltpu.VMEM((2 * LANES, 3 * LANES), jnp.bfloat16),
            pltpu.SemaphoreType.DMA((pieces,)),
            pltpu.SemaphoreType.DMA((pieces,)),
            pltpu.SemaphoreType.DMA((pieces,)),
            pltpu.SemaphoreType.DMA((chunks,)),
            pltpu.SemaphoreType.DMA((chunks,)),
            pltpu.SemaphoreType.DMA((2, pieces)),
            pltpu.SemaphoreType.DMA((len(operands),)),
        ],
        compiler_params=pltpu.CompilerParams(
            collective_id=0, has_side_effects=True, vmem_limit_bytes=56 * 1024 * 1024
        ),
    )(pltpu.with_memory_space_constraint(waveforms, pltpu.HBM), *operands)
    return pl.pallas_call(
        hand_over,
        out_shape=jax.ShapeDtypeStruct(found.shape, found.dtype),
        in_specs=[near],
        out_specs=far,
        scratch_shapes=[pltpu.SemaphoreType.DMA((4,))],
    )(pltpu.with_memory_space_constraint(found, pltpu.VMEM))


def solution(mesh):
    placed = (
        P(("grp", "apa"), "tm"),
        P(),
        P("grp"),
        P("grp"),
        P("grp"),
        P(),
        P(),
        P(),
        P(),
        P(),
        P(),
    )
    return jax.shard_map(
        local, mesh=mesh, in_specs=placed, out_specs=P("grp", ("tm", "apa")), check_vma=False
    )
```

```python
import functools
import math

import jax
import jax.numpy as jnp
import numpy as np
from jax import lax
from jax.experimental import pallas as pl
from jax.experimental.pallas import tpu as pltpu
from jax.sharding import PartitionSpec as P

LANES = 128
CHUNK = 256
MESH = pl.DeviceIdType.MESH


def rounded_up(count):
    return -(-count // LANES) * LANES


def phase_tables(wire_count):
    padded = rounded_up(wire_count)
    columns = (padded - np.arange(padded)) % wire_count

    def both(multiples):
        angle = (multiples[:, None] * columns[None, :] % wire_count) * (2.0 * math.pi / wire_count)
        return np.concatenate([np.cos(angle), np.sin(angle)], 0)

    fine, coarse = both(np.arange(LANES)), both(LANES * np.arange(8))
    return fine.astype(np.float32), coarse.astype(np.float32)


def halves(values):
    high = values.astype(jnp.bfloat16)
    return high, (values - high.astype(jnp.float32)).astype(jnp.bfloat16)


def cut(rows):
    body = rows - CHUNK
    return [(first, CHUNK) for first in range(0, body, CHUNK)] + [
        (body, CHUNK // 2),
        (body + CHUNK // 2, CHUNK // 2),
    ]


def strided(row):
    return pltpu.roll(jnp.broadcast_to(row, (LANES, LANES)), 0, 1, stride=1, stride_axis=0)


def kernel(induction, collection, waves, *refs):
    operands, out, copies = refs[:14], refs[14], refs[15:29]
    (
        halo,
        main,
        staged,
        origins,
        total,
        circulant_u,
        circulant_v,
        circulant_w,
        spread,
        folded,
        rows_h,
        kernel_rows,
        toeplitz,
        response_columns,
        next_send,
        near_send,
        far_send,
        halo_sem,
        main_sem,
        own_sem,
        fetch_sem,
    ) = refs[29:]
    (
        taps,
        slots,
        offsets,
        bad,
        induction_real,
        induction_imaginary,
        induction_filter,
        collection_real,
        collection_imaginary,
        collection_filter,
        fine_uv,
        coarse_uv,
        fine_w,
        coarse_w,
    ) = copies
    tm, apa = lax.axis_index("tm"), lax.axis_index("apa")
    windows = lax.axis_size("tm")
    following = lax.rem(tm + 1, windows)
    previous = lax.rem(tm + windows - 1, windows)
    held_rows = waves.shape[0]
    pieces = cut(held_rows)
    sizes = (induction, induction, collection)
    starts = (0, induction, 2 * induction)

    barrier = pltpu.get_barrier_semaphore()

    def greet(window, core):
        pl.semaphore_signal(
            barrier, inc=1, device_id={"tm": window, "apa": core}, device_id_type=MESH
        )

    greet(tm, 1 - apa)

    @pl.when(apa == 0)
    def _():
        greet(previous, 0)
        greet(previous, 1)

    fetches = [
        pltpu.make_async_copy(source, copy, fetch_sem.at[number])
        for number, (source, copy) in enumerate(zip(operands, copies))
    ]
    def own_halves(core):
        copies = ([], [])
        for k, (first, count) in enumerate(pieces):
            span, own = pl.ds(first, count), pl.ds(core * held_rows + first, count)
            targets = (halo.at[own], main.at[own]) if core else (main.at[own], staged.at[span])
            for half in range(2):
                source = waves.at[span, pl.ds(half * LANES, LANES)]
                copies[half].append(
                    pltpu.make_async_copy(source, targets[half], own_sem.at[half, k])
                )
        return copies

    for core in range(2):

        @pl.when(apa == core)
        def _():
            firsts, seconds = own_halves(core)
            for copy in seconds + firsts:
                copy.start()

    for fetch in fetches[:10]:
        fetch.start()
    pl.semaphore_wait(barrier, 2)

    def push(source, target, arrived, sent, window, core):
        return pltpu.make_async_remote_copy(
            src_ref=source,
            dst_ref=target,
            send_sem=sent,
            recv_sem=arrived,
            device_id={"tm": window, "apa": core},
            device_id_type=MESH,
        )

    def sends(core):
        ahead, across = [], []
        for k, (first, count) in enumerate(pieces):
            span, own = pl.ds(first, count), pl.ds(core * held_rows + first, count)
            halo_in, main_in = halo_sem.at[core, k], main_sem.at[core, k]
            second = main.at[own] if core else staged.at[span]
            ahead.append(push(second, halo.at[own], halo_in, next_send.at[k], following, 0))
            if core == 0:
                across.append(push(main.at[own], halo.at[own], halo_in, near_send.at[k], tm, 1))
                across.append(push(second, main.at[own], main_in, far_send.at[k], tm, 1))
            else:
                across.append(push(halo.at[own], main.at[own], main_in, near_send.at[k], tm, 0))
        return ahead, across

    for core in range(2):

        @pl.when(apa == core)
        def _():
            ahead, across = sends(core)
            firsts, seconds = own_halves(core)
            for copy, send in zip(seconds, ahead):
                copy.wait()
                send.start()
            for copy in firsts:
                copy.wait()
            for send in across:
                send.start()

    for fetch in fetches[10:]:
        fetch.start()
    for fetch in fetches[:10]:
        fetch.wait()

    build_rows = math.gcd(induction // 2, collection // 2)
    counted = lax.broadcasted_iota(jnp.int32, (build_rows, 2 * CHUNK), 0).astype(jnp.int16)
    one, zero = jnp.bfloat16(1), jnp.bfloat16(0)
    lane = lax.broadcasted_iota(jnp.int32, (LANES, LANES), 1)
    row_of = lax.broadcasted_iota(jnp.int32, (LANES, LANES), 0)

    def span_of(ref, first, count):
        return ref[pl.ds(pl.multiple_of(first, LANES), count)].reshape(1, count)

    def slots_of(first, count):
        def joined(ref):
            return jnp.concatenate(
                [span_of(ref, half * held_rows + first, count) for half in range(2)], 1
            )

        return jnp.where(joined(bad) == 0, joined(slots), -1)

    def plane_rows(slot, start, wires):
        hits = [
            jnp.where(counted[:, : slot.shape[1]] == (slot - first).astype(jnp.int16), one, zero)
            for first in range(start, start + wires, build_rows)
        ]
        return jnp.concatenate(hits, 0)

    def make_origins(group, carry):
        first = pl.multiple_of(group * LANES, LANES)
        delay = span_of(offsets, first, LANES).astype(jnp.float32)
        delay = jnp.broadcast_to(delay, (LANES, LANES)).T.astype(jnp.int32)
        origins[pl.ds(first, LANES), :] = (lane - delay) & (LANES - 1)
        return carry

    lax.fori_loop(0, origins.shape[0] // LANES, make_origins, 0)
    total[...] = jnp.zeros_like(total)

    spread[...] = jnp.zeros_like(spread)
    kernel_rows[...] = jnp.zeros_like(kernel_rows)
    kernel_rows[0:3, 0 : taps.shape[1]] = taps[...].astype(jnp.float32)
    for real, imaginary, gain, row in (
        (induction_real, induction_imaginary, induction_filter, 0),
        (collection_real, collection_imaginary, collection_filter, 4),
    ):
        count, width = real.shape
        re, im = real[...], imaginary[...]
        magnitude = re * re + im * im
        spread[row : row + count, 0:width] = gain[...] * re / magnitude
        spread[row + count : row + 2 * count, 0:width] = -gain[...] * im / magnitude
    for fetch in fetches[10:]:
        fetch.wait()
    for fine, coarse, count, first, targets, wires in (
        (fine_uv, coarse_uv, 2, 0, (circulant_u, circulant_v), induction),
        (fine_w, coarse_w, 1, 4, (circulant_w,), collection),
    ):
        padded = rounded_up(wires)
        blocks = padded // LANES
        for entry in range(count):
            for block in range(8):
                columns = slice(block * LANES, (block + 1) * LANES)
                re = spread[first + entry : first + entry + 1, columns]
                im = spread[first + count + entry : first + count + entry + 1, columns]
                row = 16 * entry + block
                folded[row : row + 1, 0:LANES] = re
                folded[row : row + 1, LANES : 2 * LANES] = -im
                folded[row + 8 : row + 9, 0:LANES] = im
                folded[row + 8 : row + 9, LANES : 2 * LANES] = re
        both = jnp.concatenate(halves(folded[0 : 16 * count, :]), 0)
        terms = sum(
            jnp.dot(both, table, preferred_element_type=jnp.float32) for table in halves(fine[...])
        )
        terms = terms[: 16 * count] + terms[16 * count :]
        for entry in range(count):
            re = terms[16 * entry : 16 * entry + 8]
            im = terms[16 * entry + 8 : 16 * entry + 16]
            turned = coarse[0:8, :] * re - coarse[8:16, :] * im
            line = jnp.sum(turned, axis=0, keepdims=True) * (1.0 / wires)
            rows_h[0:1, 0:padded] = line
            rows_h[0:1, wires : wires + padded] = line
            if padded > wires:
                rows_h[0:1, 2 * wires : 2 * padded] = line[:, : 2 * (padded - wires)]
            before = strided(rows_h[0:1, 0:LANES])
            for k in range(2 * blocks - 1):
                after = strided(rows_h[0:1, (k + 1) * LANES : (k + 2) * LANES])
                piece = jnp.where(lane >= row_of, after, before).astype(jnp.bfloat16)
                for i in range(targets[entry].shape[0] // LANES):
                    j = k - (blocks - 1) + i
                    if 0 <= j < blocks:
                        targets[entry][
                            i * LANES : (i + 1) * LANES, j * LANES : (j + 1) * LANES
                        ] = piece
                before = after

    for plane in range(3):
        turned = strided(kernel_rows[plane : plane + 1, :])
        columns = slice(plane * LANES, (plane + 1) * LANES)
        toeplitz[0:LANES, columns] = jnp.where(lane < row_of, turned, 0.0).astype(jnp.bfloat16)
        toeplitz[LANES : 2 * LANES, columns] = jnp.where(lane >= row_of, turned, 0.0).astype(
            jnp.bfloat16
        )

    circulants = (circulant_u, circulant_v, circulant_w)
    planes = list(zip(circulants, starts, sizes))

    def through(circulant, upper, lower):
        spare = circulant.shape[1] - 2 * upper.shape[0]
        stacked = [upper, lower]
        if spare:
            stacked.append(jnp.zeros((spare, upper.shape[1]), jnp.bfloat16))
        return jnp.dot(
            circulant[0 : upper.shape[0], :],
            jnp.concatenate(stacked, 0),
            preferred_element_type=jnp.float32,
        )

    last = len(pieces) - 1
    last_slot = slots_of(*pieces[last])
    for circulant, start, wires in planes:
        middle = start + wires // 2
        top = plane_rows(last_slot, start, wires // 2)
        bottom = plane_rows(last_slot, middle, wires // 2)
        response_columns[start:middle, :] = through(circulant, top, bottom).astype(jnp.bfloat16)
        response_columns[middle : start + wires, :] = through(circulant, bottom, top).astype(jnp.bfloat16)

    def filtered_piece(k, first, count):
        for half in range(2):
            span = pl.ds(pl.multiple_of(half * held_rows + first, LANES), count)

            @pl.when(apa != half)
            def _():
                target = main.at[span]
                pltpu.make_async_copy(target, target, main_sem.at[half, k]).wait()

            @pl.when(apa * half == 0)
            def _():
                target = halo.at[span]
                pltpu.make_async_copy(target, target, halo_sem.at[half, k]).wait()

        groups = []
        for half in range(2):
            for start in range(0, count, LANES):
                span = pl.ds(pl.multiple_of(half * held_rows + first + start, LANES), LANES)
                origin = origins[span, :]
                early = jnp.take_along_axis(halo[span, :].astype(jnp.float32), origin, axis=1)
                late = jnp.take_along_axis(main[span, :].astype(jnp.float32), origin, axis=1)
                late = jnp.where(lane >= origin, late, early)
                groups.append(jnp.concatenate([early, late], 1).astype(jnp.bfloat16))
        aligned = jnp.concatenate(groups, 0)
        return jnp.dot(aligned, toeplitz[...], preferred_element_type=jnp.float32).astype(
            jnp.bfloat16
        )

    def take(k, first, count):
        filtered = filtered_piece(k, first, count)
        slot = slots_of(first, count)
        for plane, (_, start, wires) in enumerate(planes):
            total[start : start + wires, :] += jnp.dot(
                plane_rows(slot, start, wires),
                filtered[:, plane * LANES : (plane + 1) * LANES],
                preferred_element_type=jnp.float32,
            )

    def take_whole(k, carry):
        take(k, k * CHUNK, CHUNK)
        return carry

    lax.fori_loop(0, last - 1, take_whole, 0)
    take(last - 1, *pieces[last - 1])
    for circulant, start, wires in planes:
        middle = start + wires // 2
        top = total[start:middle, :].astype(jnp.bfloat16)
        bottom = total[middle : start + wires, :].astype(jnp.bfloat16)
        values = through(
            circulant, jnp.concatenate([top, bottom], 1), jnp.concatenate([bottom, top], 1)
        )
        out[start:middle, :] = values[:, 0:LANES]
        out[middle : start + wires, :] = values[:, LANES:]
    filtered = filtered_piece(last, *pieces[last])
    for plane, (_, start, wires) in enumerate(planes):
        out[start : start + wires, :] += jnp.dot(
            response_columns[start : start + wires, :],
            filtered[:, plane * LANES : (plane + 1) * LANES],
            preferred_element_type=jnp.float32,
        )
    for core in range(2):

        @pl.when(apa == core)
        def _():
            ahead, across = sends(core)
            for copy in ahead + across:
                copy.wait_send()


def hand_over(found, out, leave):
    pieces = leave.shape[0]
    rows = found.shape[0] // pieces
    copies = [
        pltpu.make_async_copy(
            found.at[pl.ds(k * rows, rows)], out.at[pl.ds(k * rows, rows)], leave.at[k]
        )
        for k in range(pieces)
    ]
    for copy in copies:
        copy.start()
    for copy in copies:
        copy.wait()


def local(
    waveforms,
    time_kernel,
    wire_slot,
    tick_offset,
    bad_channel,
    induction_real,
    induction_imaginary,
    induction_filter,
    collection_real,
    collection_imaginary,
    collection_filter,
):
    channels = wire_slot.shape[0]
    induction, collection = induction_real.shape[1], collection_real.shape[0]
    padded_i, padded_c = rounded_up(induction), rounded_up(collection)
    half_i, half_c = rounded_up(induction // 2), rounded_up(collection // 2)
    pieces = len(cut(waveforms.shape[0]))
    operands = [
        time_kernel,
        wire_slot,
        tick_offset,
        bad_channel,
        induction_real,
        induction_imaginary,
        induction_filter,
        collection_real.reshape(1, collection),
        collection_imaginary.reshape(1, collection),
        collection_filter.reshape(1, collection),
        *map(jnp.asarray, phase_tables(induction) + phase_tables(collection)),
    ]
    far = pl.BlockSpec(memory_space=pltpu.HBM)
    near = pl.BlockSpec(memory_space=pltpu.VMEM)
    operands = [pltpu.with_memory_space_constraint(operand, pltpu.HBM) for operand in operands]
    found = pl.pallas_call(
        functools.partial(kernel, induction, collection),
        out_shape=pltpu.VMEM((channels, LANES), jnp.float32),
        in_specs=[far] * (1 + len(operands)),
        out_specs=near,
        scratch_shapes=[pltpu.VMEM(operand.shape, operand.dtype) for operand in operands]
        + [
            pltpu.VMEM((channels, LANES), jnp.bfloat16),
            pltpu.VMEM((channels, LANES), jnp.bfloat16),
            pltpu.VMEM((channels // 2, LANES), jnp.bfloat16),
            pltpu.VMEM((channels, LANES), jnp.int32),
            pltpu.VMEM((channels, LANES), jnp.float32),
            pltpu.VMEM((half_i, padded_i), jnp.bfloat16),
            pltpu.VMEM((half_i, padded_i), jnp.bfloat16),
            pltpu.VMEM((half_c, padded_c), jnp.bfloat16),
            pltpu.VMEM((8, 8 * LANES), jnp.float32),
            pltpu.VMEM((32, 2 * LANES), jnp.float32),
            pltpu.VMEM((8, 2 * max(padded_i, padded_c)), jnp.float32),
            pltpu.VMEM((8, LANES), jnp.float32),
            pltpu.VMEM((2 * LANES, 3 * LANES), jnp.bfloat16),
            pltpu.VMEM((channels, CHUNK), jnp.bfloat16),
            pltpu.SemaphoreType.DMA((pieces,)),
            pltpu.SemaphoreType.DMA((pieces,)),
            pltpu.SemaphoreType.DMA((pieces,)),
            pltpu.SemaphoreType.DMA((2, pieces)),
            pltpu.SemaphoreType.DMA((2, pieces)),
            pltpu.SemaphoreType.DMA((2, pieces)),
            pltpu.SemaphoreType.DMA((len(operands),)),
        ],
        compiler_params=pltpu.CompilerParams(
            collective_id=0, has_side_effects=True, vmem_limit_bytes=56 * 1024 * 1024
        ),
    )(pltpu.with_memory_space_constraint(waveforms, pltpu.HBM), *operands)
    return pl.pallas_call(
        hand_over,
        out_shape=jax.ShapeDtypeStruct(found.shape, found.dtype),
        in_specs=[near],
        out_specs=far,
        scratch_shapes=[pltpu.SemaphoreType.DMA((4,))],
    )(pltpu.with_memory_space_constraint(found, pltpu.VMEM))


def solution(mesh):
    placed = (
        P(("grp", "apa"), "tm"),
        P(),
        P("grp"),
        P("grp"),
        P("grp"),
        P(),
        P(),
        P(),
        P(),
        P(),
        P(),
    )
    return jax.shard_map(
        local, mesh=mesh, in_specs=placed, out_specs=P("grp", ("tm", "apa")), check_vma=False
    )
```

```python
import functools
import math

import jax
import jax.numpy as jnp
import numpy as np
from jax import lax
from jax.experimental import pallas as pl
from jax.experimental.pallas import tpu as pltpu
from jax.sharding import PartitionSpec as P

LANES = 128
CHUNK = 256
MESH = pl.DeviceIdType.MESH


def rounded_up(count):
    return -(-count // LANES) * LANES


def phase_tables(wire_count):
    padded = rounded_up(wire_count)
    columns = (padded - np.arange(padded)) % wire_count

    def both(multiples):
        angle = (multiples[:, None] * columns[None, :] % wire_count) * (2.0 * math.pi / wire_count)
        return np.concatenate([np.cos(angle), np.sin(angle)], 0)

    fine, coarse = both(np.arange(LANES)), both(LANES * np.arange(8))
    return fine.astype(np.float32), coarse.astype(np.float32)


def halves(values):
    high = values.astype(jnp.bfloat16)
    return high, (values - high.astype(jnp.float32)).astype(jnp.bfloat16)


def strided(row):
    return pltpu.roll(jnp.broadcast_to(row, (LANES, LANES)), 0, 1, stride=1, stride_axis=0)


def kernel(induction, collection, waves, *refs):
    operands, out, copies = refs[:14], refs[14], refs[15:29]
    (
        halo,
        main,
        staged,
        onehot,
        origins,
        total,
        circulant_u,
        circulant_v,
        circulant_w,
        spread,
        folded,
        rows_h,
        kernel_rows,
        toeplitz,
        next_send,
        near_send,
        far_send,
        halo_sem,
        main_sem,
        own_sem,
        fetch_sem,
    ) = refs[29:]
    (
        taps,
        slots,
        offsets,
        bad,
        induction_real,
        induction_imaginary,
        induction_filter,
        collection_real,
        collection_imaginary,
        collection_filter,
        fine_uv,
        coarse_uv,
        fine_w,
        coarse_w,
    ) = copies
    tm, apa = lax.axis_index("tm"), lax.axis_index("apa")
    windows = lax.axis_size("tm")
    following = lax.rem(tm + 1, windows)
    previous = lax.rem(tm + windows - 1, windows)
    pieces = waves.shape[0] // CHUNK
    sizes = (induction, induction, collection)
    starts = (0, induction, 2 * induction)

    barrier = pltpu.get_barrier_semaphore()

    def greet(window, core):
        pl.semaphore_signal(
            barrier, inc=1, device_id={"tm": window, "apa": core}, device_id_type=MESH
        )

    greet(tm, 1 - apa)

    @pl.when(apa == 0)
    def _():
        greet(previous, 0)
        greet(previous, 1)

    fetches = [
        pltpu.make_async_copy(source, copy, fetch_sem.at[number])
        for number, (source, copy) in enumerate(zip(operands, copies))
    ]
    def own_halves(core):
        copies = ([], [])
        for k in range(pieces):
            spot = core * pieces + k
            targets = (halo.at[spot], main.at[spot]) if core else (main.at[spot], staged.at[k])
            for half in range(2):
                source = waves.at[pl.ds(k * CHUNK, CHUNK), pl.ds(half * LANES, LANES)]
                copies[half].append(
                    pltpu.make_async_copy(source, targets[half], own_sem.at[half, k])
                )
        return copies

    for core in range(2):

        @pl.when(apa == core)
        def _():
            firsts, seconds = own_halves(core)
            for copy in seconds + firsts:
                copy.start()

    for fetch in fetches[:10]:
        fetch.start()
    pl.semaphore_wait(barrier, 2)

    def push(source, target, arrived, sent, window, core):
        return pltpu.make_async_remote_copy(
            src_ref=source,
            dst_ref=target,
            send_sem=sent,
            recv_sem=arrived,
            device_id={"tm": window, "apa": core},
            device_id_type=MESH,
        )

    def sends(core):
        ahead, across = [], []
        for k in range(pieces):
            spot = core * pieces + k
            second = main.at[spot] if core else staged.at[k]
            ahead.append(
                push(second, halo.at[spot], halo_sem.at[spot], next_send.at[k], following, 0)
            )
            if core == 0:
                across.append(
                    push(main.at[spot], halo.at[spot], halo_sem.at[spot], near_send.at[k], tm, 1)
                )
                across.append(
                    push(second, main.at[spot], main_sem.at[spot], far_send.at[k], tm, 1)
                )
            else:
                across.append(
                    push(halo.at[spot], main.at[spot], main_sem.at[spot], near_send.at[k], tm, 0)
                )
        return ahead, across

    for core in range(2):

        @pl.when(apa == core)
        def _():
            ahead, across = sends(core)
            firsts, seconds = own_halves(core)
            for copy, send in zip(seconds, ahead):
                copy.wait()
                send.start()
            for copy in firsts:
                copy.wait()
            for send in across:
                send.start()

    for fetch in fetches[10:]:
        fetch.start()
    for fetch in fetches[:10]:
        fetch.wait()

    build_rows = math.gcd(induction, collection)
    counted = lax.broadcasted_iota(jnp.int32, (build_rows, 2 * CHUNK), 0).astype(jnp.int16)
    one, zero = jnp.bfloat16(1), jnp.bfloat16(0)
    lane = lax.broadcasted_iota(jnp.int32, (LANES, LANES), 1)
    row_of = lax.broadcasted_iota(jnp.int32, (LANES, LANES), 0)

    def span_of(ref, first, count):
        return ref[pl.ds(pl.multiple_of(first, LANES), count)].reshape(1, count)

    def joined(ref, step):
        return jnp.concatenate(
            [span_of(ref, index * CHUNK, CHUNK) for index in (step, pieces + step)], 1
        )

    def plane_rows(slot, start, wires):
        hits = [
            jnp.where(counted == (slot - first).astype(jnp.int16), one, zero)
            for first in range(start, start + wires, build_rows)
        ]
        return jnp.concatenate(hits, 0)

    def make_origins(group, carry):
        first = pl.multiple_of(group * LANES, LANES)
        delay = span_of(offsets, first, LANES).astype(jnp.float32)
        delay = jnp.broadcast_to(delay, (LANES, LANES)).T.astype(jnp.int32)
        origins[pl.ds(first, LANES), :] = (lane - delay) & (LANES - 1)
        return carry

    lax.fori_loop(0, origins.shape[0] // LANES, make_origins, 0)
    total[...] = jnp.zeros_like(total)

    spread[...] = jnp.zeros_like(spread)
    kernel_rows[...] = jnp.zeros_like(kernel_rows)
    kernel_rows[0:3, 0 : taps.shape[1]] = taps[...].astype(jnp.float32)
    for real, imaginary, gain, row in (
        (induction_real, induction_imaginary, induction_filter, 0),
        (collection_real, collection_imaginary, collection_filter, 4),
    ):
        count, width = real.shape
        re, im = real[...], imaginary[...]
        magnitude = re * re + im * im
        spread[row : row + count, 0:width] = gain[...] * re / magnitude
        spread[row + count : row + 2 * count, 0:width] = -gain[...] * im / magnitude
    for fetch in fetches[10:]:
        fetch.wait()
    for fine, coarse, count, first, targets, wires in (
        (fine_uv, coarse_uv, 2, 0, (circulant_u, circulant_v), induction),
        (fine_w, coarse_w, 1, 4, (circulant_w,), collection),
    ):
        padded = rounded_up(wires)
        blocks = padded // LANES
        for entry in range(count):
            for block in range(8):
                columns = slice(block * LANES, (block + 1) * LANES)
                re = spread[first + entry : first + entry + 1, columns]
                im = spread[first + count + entry : first + count + entry + 1, columns]
                row = 16 * entry + block
                folded[row : row + 1, 0:LANES] = re
                folded[row : row + 1, LANES : 2 * LANES] = -im
                folded[row + 8 : row + 9, 0:LANES] = im
                folded[row + 8 : row + 9, LANES : 2 * LANES] = re
        both = jnp.concatenate(halves(folded[0 : 16 * count, :]), 0)
        terms = sum(
            jnp.dot(both, table, preferred_element_type=jnp.float32) for table in halves(fine[...])
        )
        terms = terms[: 16 * count] + terms[16 * count :]
        for entry in range(count):
            re = terms[16 * entry : 16 * entry + 8]
            im = terms[16 * entry + 8 : 16 * entry + 16]
            turned = coarse[0:8, :] * re - coarse[8:16, :] * im
            line = jnp.sum(turned, axis=0, keepdims=True) * (1.0 / wires)
            rows_h[0:1, 0:padded] = line
            rows_h[0:1, wires : wires + padded] = line
            if padded > wires:
                rows_h[0:1, 2 * wires : 2 * padded] = line[:, : 2 * (padded - wires)]
            before = strided(rows_h[0:1, 0:LANES])
            for k in range(2 * blocks - 1):
                after = strided(rows_h[0:1, (k + 1) * LANES : (k + 2) * LANES])
                piece = jnp.where(lane >= row_of, after, before).astype(jnp.bfloat16)
                for i in range(targets[entry].shape[0] // LANES):
                    j = k - (blocks - 1) + i
                    if 0 <= j < blocks:
                        targets[entry][
                            i * LANES : (i + 1) * LANES, j * LANES : (j + 1) * LANES
                        ] = piece
                before = after

    for plane in range(3):
        turned = strided(kernel_rows[plane : plane + 1, :])
        columns = slice(plane * LANES, (plane + 1) * LANES)
        toeplitz[0:LANES, columns] = jnp.where(lane < row_of, turned, 0.0).astype(jnp.bfloat16)
        toeplitz[LANES : 2 * LANES, columns] = jnp.where(lane >= row_of, turned, 0.0).astype(
            jnp.bfloat16
        )

    def make_onehot(step, carry):
        slot = jnp.where(joined(bad, step) == 0, joined(slots, step), -1)
        for first in range(0, total.shape[0], build_rows):
            onehot[step, first : first + build_rows, :] = plane_rows(slot, first, build_rows)
        return carry

    lax.fori_loop(0, pieces, make_onehot, 0)

    def take(step, carry):
        groups = []
        for half in range(2):
            index = half * pieces + step

            @pl.when(apa != half)
            def _():
                pltpu.make_async_copy(main.at[index], main.at[index], main_sem.at[index]).wait()

            @pl.when(apa * half == 0)
            def _():
                pltpu.make_async_copy(halo.at[index], halo.at[index], halo_sem.at[index]).wait()

        for index in (step, pieces + step):
            for start in range(0, CHUNK, LANES):
                origin = origins[
                    pl.ds(pl.multiple_of(index * CHUNK + start, LANES), LANES), :
                ]
                early = halo[index, start : start + LANES, :].astype(jnp.float32)
                late = main[index, start : start + LANES, :].astype(jnp.float32)
                early = jnp.take_along_axis(early, origin, axis=1)
                late = jnp.take_along_axis(late, origin, axis=1)
                late = jnp.where(lane >= origin, late, early)
                groups.append(jnp.concatenate([early, late], 1).astype(jnp.bfloat16))
        aligned = jnp.concatenate(groups, 0)
        filtered = jnp.dot(aligned, toeplitz[...], preferred_element_type=jnp.float32).astype(
            jnp.bfloat16
        )
        for plane, (start, wires) in enumerate(zip(starts, sizes)):
            total[start : start + wires, :] += jnp.dot(
                onehot[step, start : start + wires, :],
                filtered[:, plane * LANES : (plane + 1) * LANES],
                preferred_element_type=jnp.float32,
            )
        return carry

    lax.fori_loop(0, pieces, take, 0)

    for plane, circulant in enumerate((circulant_u, circulant_v, circulant_w)):
        start, wires = starts[plane], sizes[plane]
        half, spare = wires // 2, rounded_up(wires) - wires
        top = total[start : start + half, :].astype(jnp.bfloat16)
        bottom = total[start + half : start + wires, :].astype(jnp.bfloat16)
        stacked = [jnp.concatenate([top, bottom], 1), jnp.concatenate([bottom, top], 1)]
        if spare:
            stacked.append(jnp.zeros((spare, 2 * LANES), jnp.bfloat16))
        values = jnp.dot(
            circulant[0:half, :],
            jnp.concatenate(stacked, 0),
            preferred_element_type=jnp.float32,
        )
        out[start : start + half, :] = values[:, 0:LANES]
        out[start + half : start + wires, :] = values[:, LANES:]
    for core in range(2):

        @pl.when(apa == core)
        def _():
            ahead, across = sends(core)
            for copy in ahead + across:
                copy.wait_send()


def hand_over(found, out, leave):
    pieces = leave.shape[0]
    rows = found.shape[0] // pieces
    copies = [
        pltpu.make_async_copy(
            found.at[pl.ds(k * rows, rows)], out.at[pl.ds(k * rows, rows)], leave.at[k]
        )
        for k in range(pieces)
    ]
    for copy in copies:
        copy.start()
    for copy in copies:
        copy.wait()


def local(
    waveforms,
    time_kernel,
    wire_slot,
    tick_offset,
    bad_channel,
    induction_real,
    induction_imaginary,
    induction_filter,
    collection_real,
    collection_imaginary,
    collection_filter,
):
    channels = wire_slot.shape[0]
    induction, collection = induction_real.shape[1], collection_real.shape[0]
    padded_i, padded_c = rounded_up(induction), rounded_up(collection)
    half_i, half_c = rounded_up(induction // 2), rounded_up(collection // 2)
    chunks = channels // CHUNK
    pieces = chunks // 2
    operands = [
        time_kernel,
        wire_slot,
        tick_offset,
        bad_channel,
        induction_real,
        induction_imaginary,
        induction_filter,
        collection_real.reshape(1, collection),
        collection_imaginary.reshape(1, collection),
        collection_filter.reshape(1, collection),
        *map(jnp.asarray, phase_tables(induction) + phase_tables(collection)),
    ]
    far = pl.BlockSpec(memory_space=pltpu.HBM)
    near = pl.BlockSpec(memory_space=pltpu.VMEM)
    operands = [pltpu.with_memory_space_constraint(operand, pltpu.HBM) for operand in operands]
    found = pl.pallas_call(
        functools.partial(kernel, induction, collection),
        out_shape=pltpu.VMEM((channels, LANES), jnp.float32),
        in_specs=[far] * (1 + len(operands)),
        out_specs=near,
        scratch_shapes=[pltpu.VMEM(operand.shape, operand.dtype) for operand in operands]
        + [
            pltpu.VMEM((chunks, CHUNK, LANES), jnp.bfloat16),
            pltpu.VMEM((chunks, CHUNK, LANES), jnp.bfloat16),
            pltpu.VMEM((pieces, CHUNK, LANES), jnp.bfloat16),
            pltpu.VMEM((pieces, channels, 2 * CHUNK), jnp.bfloat16),
            pltpu.VMEM((channels, LANES), jnp.int32),
            pltpu.VMEM((channels, LANES), jnp.float32),
            pltpu.VMEM((half_i, padded_i), jnp.bfloat16),
            pltpu.VMEM((half_i, padded_i), jnp.bfloat16),
            pltpu.VMEM((half_c, padded_c), jnp.bfloat16),
            pltpu.VMEM((8, 8 * LANES), jnp.float32),
            pltpu.VMEM((32, 2 * LANES), jnp.float32),
            pltpu.VMEM((8, 2 * max(padded_i, padded_c)), jnp.float32),
            pltpu.VMEM((8, LANES), jnp.float32),
            pltpu.VMEM((2 * LANES, 3 * LANES), jnp.bfloat16),
            pltpu.SemaphoreType.DMA((pieces,)),
            pltpu.SemaphoreType.DMA((pieces,)),
            pltpu.SemaphoreType.DMA((pieces,)),
            pltpu.SemaphoreType.DMA((chunks,)),
            pltpu.SemaphoreType.DMA((chunks,)),
            pltpu.SemaphoreType.DMA((2, pieces)),
            pltpu.SemaphoreType.DMA((len(operands),)),
        ],
        compiler_params=pltpu.CompilerParams(
            collective_id=0, has_side_effects=True, vmem_limit_bytes=56 * 1024 * 1024
        ),
    )(pltpu.with_memory_space_constraint(waveforms, pltpu.HBM), *operands)
    return pl.pallas_call(
        hand_over,
        out_shape=jax.ShapeDtypeStruct(found.shape, found.dtype),
        in_specs=[near],
        out_specs=far,
        scratch_shapes=[pltpu.SemaphoreType.DMA((4,))],
    )(pltpu.with_memory_space_constraint(found, pltpu.VMEM))


def solution(mesh):
    placed = (
        P(("grp", "apa"), "tm"),
        P(),
        P("grp"),
        P("grp"),
        P("grp"),
        P(),
        P(),
        P(),
        P(),
        P(),
        P(),
    )
    return jax.shard_map(
        local, mesh=mesh, in_specs=placed, out_specs=P("grp", ("tm", "apa")), check_vma=False
    )
```

```python
import functools
import math

import jax
import jax.numpy as jnp
import numpy as np
from jax import lax
from jax.experimental import pallas as pl
from jax.experimental.pallas import tpu as pltpu
from jax.sharding import PartitionSpec as P

LANES = 128
CHUNK = 256
MESH = pl.DeviceIdType.MESH


def rounded_up(count):
    return -(-count // LANES) * LANES


def phase_tables(wire_count):
    padded = rounded_up(wire_count)
    columns = (padded - np.arange(padded)) % wire_count

    def both(multiples):
        angle = (multiples[:, None] * columns[None, :] % wire_count) * (2.0 * math.pi / wire_count)
        return np.concatenate([np.cos(angle), np.sin(angle)], 0)

    fine, coarse = both(np.arange(LANES)), both(LANES * np.arange(8))
    return fine.astype(np.float32), coarse.astype(np.float32)


def halves(values):
    high = values.astype(jnp.bfloat16)
    return high, (values - high.astype(jnp.float32)).astype(jnp.bfloat16)


def strided(row):
    return pltpu.roll(jnp.broadcast_to(row, (LANES, LANES)), 0, 1, stride=1, stride_axis=0)


def kernel(induction, collection, waves, *refs):
    operands, found, copies = refs[:14], refs[14:18], refs[18:32]
    total, circulant_u, circulant_v, circulant_w = found
    (
        halo,
        main,
        staged,
        origins,
        spread,
        folded,
        rows_h,
        kernel_rows,
        toeplitz,
        next_send,
        near_send,
        far_send,
        halo_sem,
        main_sem,
        own_sem,
        fetch_sem,
    ) = refs[32:]
    (
        taps,
        slots,
        offsets,
        bad,
        induction_real,
        induction_imaginary,
        induction_filter,
        collection_real,
        collection_imaginary,
        collection_filter,
        fine_uv,
        coarse_uv,
        fine_w,
        coarse_w,
    ) = copies
    tm, apa = lax.axis_index("tm"), lax.axis_index("apa")
    windows = lax.axis_size("tm")
    following = lax.rem(tm + 1, windows)
    previous = lax.rem(tm + windows - 1, windows)
    pieces = waves.shape[0] // CHUNK
    sizes = (induction, induction, collection)
    starts = (0, induction, 2 * induction)

    barrier = pltpu.get_barrier_semaphore()

    def greet(window, core):
        pl.semaphore_signal(
            barrier, inc=1, device_id={"tm": window, "apa": core}, device_id_type=MESH
        )

    greet(tm, 1 - apa)

    @pl.when(apa == 0)
    def _():
        greet(previous, 0)
        greet(previous, 1)

    fetches = [
        pltpu.make_async_copy(source, copy, fetch_sem.at[number])
        for number, (source, copy) in enumerate(zip(operands, copies))
    ]
    def own_halves(core):
        copies = ([], [])
        for k in range(pieces):
            spot = core * pieces + k
            targets = (halo.at[spot], main.at[spot]) if core else (main.at[spot], staged.at[k])
            for half in range(2):
                source = waves.at[pl.ds(k * CHUNK, CHUNK), pl.ds(half * LANES, LANES)]
                copies[half].append(
                    pltpu.make_async_copy(source, targets[half], own_sem.at[half, k])
                )
        return copies

    for core in range(2):

        @pl.when(apa == core)
        def _():
            firsts, seconds = own_halves(core)
            for copy in seconds + firsts:
                copy.start()

    for fetch in fetches[:10]:
        fetch.start()
    pl.semaphore_wait(barrier, 2)

    def push(source, target, arrived, sent, window, core):
        return pltpu.make_async_remote_copy(
            src_ref=source,
            dst_ref=target,
            send_sem=sent,
            recv_sem=arrived,
            device_id={"tm": window, "apa": core},
            device_id_type=MESH,
        )

    def sends(core):
        ahead, across = [], []
        for k in range(pieces):
            spot = core * pieces + k
            second = main.at[spot] if core else staged.at[k]
            ahead.append(
                push(second, halo.at[spot], halo_sem.at[spot], next_send.at[k], following, 0)
            )
            if core == 0:
                across.append(
                    push(main.at[spot], halo.at[spot], halo_sem.at[spot], near_send.at[k], tm, 1)
                )
                across.append(
                    push(second, main.at[spot], main_sem.at[spot], far_send.at[k], tm, 1)
                )
            else:
                across.append(
                    push(halo.at[spot], main.at[spot], main_sem.at[spot], near_send.at[k], tm, 0)
                )
        return ahead, across

    for core in range(2):

        @pl.when(apa == core)
        def _():
            ahead, across = sends(core)
            firsts, seconds = own_halves(core)
            for copy, send in zip(seconds, ahead):
                copy.wait()
                send.start()
            for copy in firsts:
                copy.wait()
            for send in across:
                send.start()

    for fetch in fetches[10:]:
        fetch.start()
    for fetch in fetches[:10]:
        fetch.wait()

    build_rows = math.gcd(induction, collection)
    counted = lax.broadcasted_iota(jnp.int32, (build_rows, 2 * CHUNK), 0).astype(jnp.int16)
    one, zero = jnp.bfloat16(1), jnp.bfloat16(0)
    lane = lax.broadcasted_iota(jnp.int32, (LANES, LANES), 1)
    row_of = lax.broadcasted_iota(jnp.int32, (LANES, LANES), 0)

    def span_of(ref, first, count):
        return ref[pl.ds(pl.multiple_of(first, LANES), count)].reshape(1, count)

    def joined(ref, step):
        return jnp.concatenate(
            [span_of(ref, index * CHUNK, CHUNK) for index in (step, pieces + step)], 1
        )

    def plane_rows(slot, start, wires):
        hits = [
            jnp.where(counted == (slot - first).astype(jnp.int16), one, zero)
            for first in range(start, start + wires, build_rows)
        ]
        return jnp.concatenate(hits, 0)

    def make_origins(group, carry):
        first = pl.multiple_of(group * LANES, LANES)
        delay = span_of(offsets, first, LANES).astype(jnp.float32)
        delay = jnp.broadcast_to(delay, (LANES, LANES)).T.astype(jnp.int32)
        origins[pl.ds(first, LANES), :] = (lane - delay) & (LANES - 1)
        return carry

    lax.fori_loop(0, origins.shape[0] // LANES, make_origins, 0)
    total[...] = jnp.zeros_like(total)

    spread[...] = jnp.zeros_like(spread)
    kernel_rows[...] = jnp.zeros_like(kernel_rows)
    kernel_rows[0:3, 0 : taps.shape[1]] = taps[...].astype(jnp.float32)
    for real, imaginary, gain, row in (
        (induction_real, induction_imaginary, induction_filter, 0),
        (collection_real, collection_imaginary, collection_filter, 4),
    ):
        count, width = real.shape
        re, im = real[...], imaginary[...]
        magnitude = re * re + im * im
        spread[row : row + count, 0:width] = gain[...] * re / magnitude
        spread[row + count : row + 2 * count, 0:width] = -gain[...] * im / magnitude
    for fetch in fetches[10:]:
        fetch.wait()
    for fine, coarse, count, first, targets, wires in (
        (fine_uv, coarse_uv, 2, 0, (circulant_u, circulant_v), induction),
        (fine_w, coarse_w, 1, 4, (circulant_w,), collection),
    ):
        padded = rounded_up(wires)
        blocks = padded // LANES
        for entry in range(count):
            for block in range(8):
                columns = slice(block * LANES, (block + 1) * LANES)
                re = spread[first + entry : first + entry + 1, columns]
                im = spread[first + count + entry : first + count + entry + 1, columns]
                row = 16 * entry + block
                folded[row : row + 1, 0:LANES] = re
                folded[row : row + 1, LANES : 2 * LANES] = -im
                folded[row + 8 : row + 9, 0:LANES] = im
                folded[row + 8 : row + 9, LANES : 2 * LANES] = re
        both = jnp.concatenate(halves(folded[0 : 16 * count, :]), 0)
        terms = sum(
            jnp.dot(both, table, preferred_element_type=jnp.float32) for table in halves(fine[...])
        )
        terms = terms[: 16 * count] + terms[16 * count :]
        for entry in range(count):
            re = terms[16 * entry : 16 * entry + 8]
            im = terms[16 * entry + 8 : 16 * entry + 16]
            turned = coarse[0:8, :] * re - coarse[8:16, :] * im
            line = jnp.sum(turned, axis=0, keepdims=True) * (1.0 / wires)
            rows_h[0:1, 0:padded] = line
            rows_h[0:1, wires : wires + padded] = line
            if padded > wires:
                rows_h[0:1, 2 * wires : 2 * padded] = line[:, : 2 * (padded - wires)]
            before = strided(rows_h[0:1, 0:LANES])
            for k in range(2 * blocks - 1):
                after = strided(rows_h[0:1, (k + 1) * LANES : (k + 2) * LANES])
                piece = jnp.where(lane >= row_of, after, before).astype(jnp.bfloat16)
                for i in range(targets[entry].shape[0] // LANES):
                    j = k - (blocks - 1) + i
                    if 0 <= j < blocks:
                        targets[entry][
                            i * LANES : (i + 1) * LANES, j * LANES : (j + 1) * LANES
                        ] = piece
                before = after

    for plane in range(3):
        turned = strided(kernel_rows[plane : plane + 1, :])
        columns = slice(plane * LANES, (plane + 1) * LANES)
        toeplitz[0:LANES, columns] = jnp.where(lane < row_of, turned, 0.0).astype(jnp.bfloat16)
        toeplitz[LANES : 2 * LANES, columns] = jnp.where(lane >= row_of, turned, 0.0).astype(
            jnp.bfloat16
        )

    def take(step, carry):
        groups = []
        for half in range(2):
            index = half * pieces + step

            @pl.when(apa != half)
            def _():
                pltpu.make_async_copy(main.at[index], main.at[index], main_sem.at[index]).wait()

            @pl.when(apa * half == 0)
            def _():
                pltpu.make_async_copy(halo.at[index], halo.at[index], halo_sem.at[index]).wait()

        for index in (step, pieces + step):
            for start in range(0, CHUNK, LANES):
                origin = origins[
                    pl.ds(pl.multiple_of(index * CHUNK + start, LANES), LANES), :
                ]
                early = halo[index, start : start + LANES, :].astype(jnp.float32)
                late = main[index, start : start + LANES, :].astype(jnp.float32)
                early = jnp.take_along_axis(early, origin, axis=1)
                late = jnp.take_along_axis(late, origin, axis=1)
                late = jnp.where(lane >= origin, late, early)
                groups.append(jnp.concatenate([early, late], 1).astype(jnp.bfloat16))
        slot = jnp.where(joined(bad, step) == 0, joined(slots, step), -1)
        aligned = jnp.concatenate(groups, 0)
        filtered = jnp.dot(aligned, toeplitz[...], preferred_element_type=jnp.float32).astype(
            jnp.bfloat16
        )
        for plane, (start, wires) in enumerate(zip(starts, sizes)):
            total[start : start + wires, :] += jnp.dot(
                plane_rows(slot, start, wires),
                filtered[:, plane * LANES : (plane + 1) * LANES],
                preferred_element_type=jnp.float32,
            )
        return carry

    lax.fori_loop(0, pieces, take, 0)

    for core in range(2):

        @pl.when(apa == core)
        def _():
            ahead, across = sends(core)
            for copy in ahead + across:
                copy.wait_send()


def respond(
    sizes, total, circulant_u, circulant_v, circulant_w, out, result, leave
):
    place, copies = 0, []
    for plane, circulant in enumerate((circulant_u, circulant_v, circulant_w)):
        wires = sizes[plane]
        half, spare = wires // 2, circulant.shape[1] - wires
        top = total[place : place + half, :].astype(jnp.bfloat16)
        bottom = total[place + half : place + wires, :].astype(jnp.bfloat16)
        stacked = [jnp.concatenate([top, bottom], 1), jnp.concatenate([bottom, top], 1)]
        if spare:
            stacked.append(jnp.zeros((spare, 2 * LANES), jnp.bfloat16))
        values = jnp.dot(
            circulant[0:half, :],
            jnp.concatenate(stacked, 0),
            preferred_element_type=jnp.float32,
        )
        result[place : place + half, :] = values[:, 0:LANES]
        result[place + half : place + wires, :] = values[:, LANES:]
        span = pl.ds(place, wires)
        copies.append(pltpu.make_async_copy(result.at[span], out.at[span], leave.at[plane]))
        copies[-1].start()
        place += wires
    for copy in copies:
        copy.wait()


def local(
    waveforms,
    time_kernel,
    wire_slot,
    tick_offset,
    bad_channel,
    induction_real,
    induction_imaginary,
    induction_filter,
    collection_real,
    collection_imaginary,
    collection_filter,
):
    channels = wire_slot.shape[0]
    induction, collection = induction_real.shape[1], collection_real.shape[0]
    padded_i, padded_c = rounded_up(induction), rounded_up(collection)
    half_i, half_c = rounded_up(induction // 2), rounded_up(collection // 2)
    chunks = channels // CHUNK
    pieces = chunks // 2
    operands = [
        time_kernel,
        wire_slot,
        tick_offset,
        bad_channel,
        induction_real,
        induction_imaginary,
        induction_filter,
        collection_real.reshape(1, collection),
        collection_imaginary.reshape(1, collection),
        collection_filter.reshape(1, collection),
        *map(jnp.asarray, phase_tables(induction) + phase_tables(collection)),
    ]
    far = pl.BlockSpec(memory_space=pltpu.HBM)
    near = pl.BlockSpec(memory_space=pltpu.VMEM)
    operands = [pltpu.with_memory_space_constraint(operand, pltpu.HBM) for operand in operands]
    found = pl.pallas_call(
        functools.partial(kernel, induction, collection),
        out_shape=[
            pltpu.VMEM((channels, LANES), jnp.float32),
            pltpu.VMEM((half_i, padded_i), jnp.bfloat16),
            pltpu.VMEM((half_i, padded_i), jnp.bfloat16),
            pltpu.VMEM((half_c, padded_c), jnp.bfloat16),
        ],
        in_specs=[far] * (1 + len(operands)),
        out_specs=[near] * 4,
        scratch_shapes=[pltpu.VMEM(operand.shape, operand.dtype) for operand in operands]
        + [
            pltpu.VMEM((chunks, CHUNK, LANES), jnp.bfloat16),
            pltpu.VMEM((chunks, CHUNK, LANES), jnp.bfloat16),
            pltpu.VMEM((pieces, CHUNK, LANES), jnp.bfloat16),
            pltpu.VMEM((channels, LANES), jnp.int32),
            pltpu.VMEM((8, 8 * LANES), jnp.float32),
            pltpu.VMEM((32, 2 * LANES), jnp.float32),
            pltpu.VMEM((8, 2 * max(padded_i, padded_c)), jnp.float32),
            pltpu.VMEM((8, LANES), jnp.float32),
            pltpu.VMEM((2 * LANES, 3 * LANES), jnp.bfloat16),
            pltpu.SemaphoreType.DMA((pieces,)),
            pltpu.SemaphoreType.DMA((pieces,)),
            pltpu.SemaphoreType.DMA((pieces,)),
            pltpu.SemaphoreType.DMA((chunks,)),
            pltpu.SemaphoreType.DMA((chunks,)),
            pltpu.SemaphoreType.DMA((2, pieces)),
            pltpu.SemaphoreType.DMA((len(operands),)),
        ],
        compiler_params=pltpu.CompilerParams(
            collective_id=0, has_side_effects=True, vmem_limit_bytes=56 * 1024 * 1024
        ),
    )(pltpu.with_memory_space_constraint(waveforms, pltpu.HBM), *operands)
    return pl.pallas_call(
        functools.partial(respond, (induction, induction, collection)),
        out_shape=jax.ShapeDtypeStruct((channels, LANES), jnp.float32),
        in_specs=[near] * 4,
        out_specs=far,
        scratch_shapes=[
            pltpu.VMEM((channels, LANES), jnp.float32),
            pltpu.SemaphoreType.DMA((3,)),
        ],
        compiler_params=pltpu.CompilerParams(vmem_limit_bytes=32 * 1024 * 1024),
    )(*[pltpu.with_memory_space_constraint(array, pltpu.VMEM) for array in found])


def solution(mesh):
    placed = (
        P(("grp", "apa"), "tm"),
        P(),
        P("grp"),
        P("grp"),
        P("grp"),
        P(),
        P(),
        P(),
        P(),
        P(),
        P(),
    )
    return jax.shard_map(
        local, mesh=mesh, in_specs=placed, out_specs=P("grp", ("tm", "apa")), check_vma=False
    )
```
